128 devices in a mesh: seq: 16 (over x, y), leaf: 8 (over z, core).
Axes of the slice: x: 4, y: 4, z: 4, core: 2. Of those that a mesh axis runs over, the one named last changes fastest.
Arguments:
- prompt_x: bfloat16 [8, 8192, 4096], P('leaf', 'seq'), may hold values from -6 to 6
- prompt_dt: float32 [8, 8192, 64], P('leaf', 'seq')
- head_rate: float32 [64], replicated
- prompt_b: bfloat16 [8, 8192, 512], P('leaf', 'seq'), may hold values from -6 to 6
- prompt_c: bfloat16 [8, 8192, 512], P('leaf', 'seq'), may hold values from -0.75 to 0.75
- prompt_dy: bfloat16 [8, 8192, 4096], P('leaf', 'seq'), may hold values from -3 to 3
- branch_x: bfloat16 [128, 256, 4096], P(('seq', 'leaf')), may hold values from -6 to 6
- branch_dt: float32 [128, 256, 64], P(('seq', 'leaf'))
- branch_b: bfloat16 [128, 256, 512], P(('seq', 'leaf')), may hold values from -6 to 6
- branch_c: bfloat16 [128, 256, 512], P(('seq', 'leaf')), may hold values from -0.75 to 0.75
- branch_dy: bfloat16 [128, 256, 4096], P(('seq', 'leaf')), may hold values from -3 to 3
- parent: int32 [128], P(('seq', 'leaf')), may hold values from 0 to 7
- lengths: int32 [128], P(('seq', 'leaf')), may hold values from 1 to 256, 16640 in all
Outputs:
- prompt_dx: bfloat16 [8, 8192, 4096], P('leaf', 'seq')
- prompt_db: bfloat16 [8, 8192, 512], P('leaf', 'seq')
- prompt_dc: bfloat16 [8, 8192, 512], P('leaf', 'seq')
- branch_dx: bfloat16 [128, 256, 4096], P(('seq', 'leaf'))
- branch_db: bfloat16 [128, 256, 512], P(('seq', 'leaf'))
- branch_dc: bfloat16 [128, 256, 512], P(('seq', 'leaf'))
The draws below stay inside these ranges and needn't reach their ends.
All inputs are finite; a program needn't handle non-finite values. No bound on the sum of `lengths` on one device may be relied on, other than what follows from the above.
Results may differ from the reference program's by a relative error of at most 0.001.
Values sent between devices are 32-bit elements; how exact they have to be, the bound alone decides.
No kernel may reach another device: no remote copies, remote signals or barrier semaphores. Data moves between devices by JAX's collectives and lax.ppermute only.
A program may use at most 192 MiB of HBM per device.

```python
import math
import jax
import jax.numpy as jnp
import numpy as np
from jax import lax

H = 64
P_SIZE = 64
N = 64
G = 8
SEGLEN = 512
BLEN = 256
PLEN = 8192
PROMPTS = 8
BRANCHES = 128


def head_rates(key, share):
    pick = jax.random.uniform(jax.random.fold_in(key, 101), (H,))
    slow = pick < share
    span = SEGLEN * jnp.exp(jax.random.uniform(jax.random.fold_in(key, 102), (H,), minval=math.log(0.04), maxval=math.log(0.16)))
    reach = jnp.exp(jax.random.uniform(jax.random.fold_in(key, 103), (H,), minval=math.log(0.3), maxval=math.log(1.2)))
    scale = jnp.where(slow, 1.5 / math.sqrt(PLEN), 1.5 / jnp.sqrt(span))
    decay_rate = jnp.where(slow, reach / (scale * PLEN), 1.0 / (scale * span))
    return (scale, decay_rate)


def draw_head_rate(key, part):
    share = 0.5
    scale, decay_rate = head_rates(key, share)
    return decay_rate.astype(jnp.float32)


def draw_prompt_dt(key, part):
    share = 0.5
    scale, decay_rate = head_rates(key, share)
    key = jax.random.fold_in(key, 1)
    jitter = jnp.exp(jax.random.uniform(jax.random.fold_in(key, 2), (PROMPTS, PLEN, H), minval=-math.log(2.0), maxval=math.log(2.0)))
    blocks = jnp.exp(jax.random.uniform(jax.random.fold_in(key, 3), (PROMPTS, PLEN // SEGLEN, 1), minval=-math.log(2.0), maxval=math.log(2.0)))
    blocks = jnp.repeat(blocks, SEGLEN, axis=1)
    return (scale[None, None, :] * jitter * blocks).astype(jnp.float32)


def draw_branch_dt(key, part):
    share = 0.5
    scale, decay_rate = head_rates(key, share)
    key = jax.random.fold_in(key, 5)
    jitter = jnp.exp(jax.random.uniform(jax.random.fold_in(key, 6), (BRANCHES, BLEN, H), minval=-math.log(2.0), maxval=math.log(2.0)))
    factor = jnp.exp(jax.random.uniform(jax.random.fold_in(key, 7), (BRANCHES, 1, 1), minval=-math.log(2.0), maxval=math.log(2.0)))
    return (scale[None, None, :] * jitter * factor).astype(jnp.float32)


def place_ends(values, key, smallest, top_value):
    extent = values.shape
    spot = [jax.random.randint(jax.random.fold_in(key, axis), (), 0, extent[axis]) for axis in range(len(extent))]
    values = values.at[tuple(spot)].set(smallest)
    longest = extent.index(max(extent))
    spot[longest] = (spot[longest] + 1) % extent[longest]
    return values.at[tuple(spot)].set(top_value)


def steps_of(stream_key, extent, cuts, least, top_value):
    factor_of = 1.0
    for axis_at, shards_of in cuts:
        heights = jax.random.uniform(jax.random.fold_in(jax.random.fold_in(stream_key, 6), axis_at), (shards_of,), jnp.float32, least / len(cuts), top_value / len(cuts))
        factor_of = factor_of * jnp.repeat(jnp.exp(heights), extent[axis_at] // shards_of).reshape((-1,) + (1,) * (len(extent) - 1 - axis_at))
    return factor_of


def cumulative_ranks(amount, lean):
    weights = [(1 << 20) // math.isqrt(rank ** lean) + 1 for rank in range(1, amount + 1)]
    scale = 1 + sum(weights) // (1 << 30)
    return np.cumsum(np.array([max(1, weight // scale) for weight in weights]))


def ranked_ids(stream_key, dims, number_of, slope):
    grid = cumulative_ranks(number_of, slope)
    ticket = jax.random.randint(jax.random.fold_in(stream_key, 1), dims, 0, int(grid[number_of - 1]))
    grade = jnp.searchsorted(jnp.asarray(grid, jnp.int32), ticket, side="right")
    return jax.random.permutation(jax.random.fold_in(stream_key, 2), number_of)[grade].astype(jnp.int32)


def profile(amount, total, limit, skew):
    weights = [(1 << 20) // math.isqrt(rank ** skew) + 1 for rank in range(2, amount + 1)]
    spare, counts = total - limit - (amount - 1), [1] * (amount - 1)
    while spare > 0:
        free = [i for i in range(amount - 1) if counts[i] < limit]
        mass, left = sum([weights[i] for i in free]), spare
        for i in free:
            extra = min(limit - counts[i], max(1, left * weights[i] // mass), spare)
            counts[i] = counts[i] + extra
            spare = spare - extra
    return np.array([limit] + counts)


def ragged(own_key, number_of, total, limit, slope):
    if number_of == 2:
        one = jax.random.randint(own_key, (), max(1, total - limit), min(limit, total - 1) + 1)
        return jnp.stack([one, total - one])
    sizes = jnp.asarray(profile(number_of, total, limit, slope), jnp.int32)
    pairs = (number_of - 1) // 2
    giver, taker = sizes[1:1 + 2 * pairs:2], sizes[2:2 + 2 * pairs:2]
    slack = jnp.minimum(giver - 1, limit - taker)
    passed = jax.random.randint(jax.random.fold_in(own_key, 1), (pairs,), 0, 1 << 20) % (slack + 1)
    sizes = sizes.at[1:1 + 2 * pairs:2].set(giver - passed).at[2:2 + 2 * pairs:2].set(taker + passed)
    return sizes[jax.random.permutation(jax.random.fold_in(own_key, 2), number_of)]


def gaussian(key, dims, scale, most, shards=(), kind=jnp.bfloat16):
    drawn = scale * jax.random.normal(key, dims, jnp.float32)
    if shards:
        drawn = drawn * steps_of(key, dims, shards, -0.22, 0.18)
    return jnp.clip(drawn, -most, most).astype(kind)


def setup_inputs(seed: int = 0) -> dict:
    key_of = jax.random.split(jax.random.key(seed), 14)
    prompt_x = gaussian(key_of[0], (PROMPTS, PLEN, H * P_SIZE), 1.0, 6.0, ((0, 8), (1, 16)))
    prompt_dt = draw_prompt_dt(jax.random.fold_in(key_of[13], 71), 0)
    head_rate = draw_head_rate(jax.random.fold_in(key_of[13], 71), 0)
    prompt_b = gaussian(key_of[3], (PROMPTS, PLEN, G * N), 1.0, 6.0, ((0, 8), (1, 16)))
    prompt_c = gaussian(key_of[4], (PROMPTS, PLEN, G * N), 0.125, 0.75, ((0, 8), (1, 16)))
    prompt_dy = gaussian(key_of[5], (PROMPTS, PLEN, H * P_SIZE), 0.5, 3.0, ((0, 8), (1, 16)))
    branch_x = gaussian(key_of[6], (BRANCHES, BLEN, H * P_SIZE), 1.0, 6.0, ((0, 128),))
    branch_dt = draw_branch_dt(jax.random.fold_in(key_of[13], 71), 0)
    branch_b = gaussian(key_of[8], (BRANCHES, BLEN, G * N), 1.0, 6.0, ((0, 128),))
    branch_c = gaussian(key_of[9], (BRANCHES, BLEN, G * N), 0.125, 0.75, ((0, 128),))
    branch_dy = gaussian(key_of[10], (BRANCHES, BLEN, H * P_SIZE), 0.5, 3.0, ((0, 128),))
    parent = place_ends(ranked_ids(key_of[11], (BRANCHES,), PROMPTS, 1), jax.random.fold_in(key_of[11], 3), 0, PROMPTS - 1).astype(jnp.int32)
    lengths = ragged(key_of[12], BRANCHES, BRANCHES * BLEN // 2 + BLEN, BLEN, 0).astype(jnp.int32)
    return {"prompt_x": prompt_x, "prompt_dt": prompt_dt, "head_rate": head_rate, "prompt_b": prompt_b, "prompt_c": prompt_c, "prompt_dy": prompt_dy, "branch_x": branch_x, "branch_dt": branch_dt, "branch_b": branch_b, "branch_c": branch_c, "branch_dy": branch_dy, "parent": parent, "lengths": lengths}


highest = lax.Precision.HIGHEST

def segment(inputs, step_rates, head_rate, b_proj, c_proj, initial):
    length = inputs.shape[0]
    head_count = step_rates.shape[1]
    head_width = initial.shape[1]
    states = initial.shape[2]
    groups = b_proj.shape[1] // states
    per_group = head_count // groups
    cumlog = jnp.cumsum(-step_rates * head_rate[None, :], axis=0)
    x_groups = inputs.reshape(length, groups, per_group, head_width).transpose(1, 0, 2, 3)
    b_groups = b_proj.reshape(length, groups, states).transpose(1, 0, 2)
    c_groups = c_proj.reshape(length, groups, states).transpose(1, 0, 2)
    cum_groups = cumlog.reshape(length, groups, per_group).transpose(1, 0, 2)
    rate_groups = step_rates.reshape(length, groups, per_group).transpose(1, 0, 2)
    init_groups = initial.reshape(groups, per_group, head_width, states)
    positions = jnp.arange(length)
    causal = (positions[:, None] >= positions[None, :])[None]

    def one_group(packed):
        x_one, b_one, c_one, cum_one, rate_one, init_one = packed
        scores = jnp.dot(c_one, b_one.T, precision=highest)
        spread = cum_one.T[:, :, None] - cum_one.T[:, None, :]
        decays = jnp.where(causal, jnp.exp(jnp.where(causal, spread, 0.0)), 0.0)
        weights = decays * scores[None] * rate_one.T[:, None, :]
        output = jnp.einsum('hts,shp->thp', weights, x_one, precision=highest)
        carried = jnp.einsum('tn,hpn->thp', c_one, init_one, precision=highest)
        output = output + jnp.exp(cum_one)[:, :, None] * carried
        final_log = cum_one[-1]
        weighting = jnp.exp(final_log[None, :] - cum_one) * rate_one
        closing = jnp.exp(final_log)[:, None, None] * init_one + jnp.einsum('shp,sn->hpn', weighting[:, :, None] * x_one, b_one, precision=highest)
        return (output, closing)
    outputs, closings = lax.map(jax.checkpoint(one_group), (x_groups, b_groups, c_groups, cum_groups, rate_groups, init_groups))
    return (outputs.transpose(1, 0, 2, 3).reshape(length, head_count * head_width), closings.reshape(head_count, head_width, states))

def prompt_pass(inputs, step_rates, head_rate, b_proj, c_proj):
    blocks = inputs.shape[0] // SEGLEN

    def split(array):
        return array.reshape((blocks, SEGLEN) + array.shape[1:])

    def advance_plain(carry, packed):
        x_in, rate_in, b_in, c_in = packed
        output, closing = segment(x_in, rate_in, head_rate, b_in, c_in, carry)
        return (closing, output)
    advance = jax.checkpoint(advance_plain)
    zero_state = jnp.zeros((H, P_SIZE, N), jnp.float32)
    closing, outputs = lax.scan(advance, zero_state, (split(inputs), split(step_rates), split(b_proj), split(c_proj)))
    return (outputs.reshape(inputs.shape[0], H * P_SIZE), closing)

def reference(prompt_x, prompt_dt, head_rate, prompt_b, prompt_c, prompt_dy, branch_x, branch_dt, branch_b, branch_c, branch_dy, parent, lengths):
    live = (jnp.arange(BLEN)[None, :] < lengths[:, None]).astype(jnp.float32)
    branch_rates = branch_dt * live[:, :, None]

    def prompt_one(packed):
        return prompt_pass(packed[0], packed[1], head_rate, packed[2], packed[3])

    def branch_plain(packed):
        return segment(packed[0], packed[1], head_rate, packed[2], packed[3], packed[4])[0]
    branch_one = jax.checkpoint(branch_plain)

    def forward(prompt_in, prompt_bin, prompt_cin, branch_in, branch_bin, branch_cin):
        prompt_y, prompt_end = lax.map(prompt_one, (prompt_in, prompt_dt, prompt_bin, prompt_cin))
        branch_start = prompt_end[parent]
        branch_y = lax.map(branch_one, (branch_in, branch_rates, branch_bin, branch_cin, branch_start))
        return (prompt_y, branch_y)
    _, pullback = jax.vjp(forward, prompt_x.astype(jnp.float32), prompt_b.astype(jnp.float32), prompt_c.astype(jnp.float32), branch_x.astype(jnp.float32), branch_b.astype(jnp.float32), branch_c.astype(jnp.float32))
    grads = pullback((prompt_dy.astype(jnp.float32), branch_dy.astype(jnp.float32) * live[:, :, None]))
    return (grads[0].astype(jnp.bfloat16), grads[1].astype(jnp.bfloat16), grads[2].astype(jnp.bfloat16), grads[3].astype(jnp.bfloat16), grads[4].astype(jnp.bfloat16), grads[5].astype(jnp.bfloat16))
```

```python
import functools
import math

import jax
import jax.numpy as jnp
from jax import lax
from jax.experimental import pallas as pl
from jax.experimental.pallas import tpu as pltpu
from jax.sharding import PartitionSpec as P

P_SIZE = 64
N = 64
CH = 128
LOG2E = math.log2(math.e)
F32 = jnp.float32
BF16 = jnp.bfloat16
ROWS = 200
HIGHEST = lax.Precision.HIGHEST


def split(value):
    hi = value.astype(BF16)
    return hi, (value - hi.astype(F32)).astype(BF16)


def dot(a, b, ca, cb):
    return lax.dot_general(a, b, (((ca,), (cb,)), ((), ())), preferred_element_type=F32)


def halves(rows):
    return lax.broadcasted_iota(jnp.int32, (rows, 128), 1) < 64


def summary_kernel(
    x_ref, dy_ref, b_ref, c_ref, wt_ref, et_ref, ydy_ref, yc_ref, yet_ref, row_ref, out_ref
):
    first = halves(64)

    def one(proj, weight_ref, value_ref, base):
        proj_t = proj.astype(F32).T
        for k in range(8):
            part = proj_t[(k // 4) * 64 : (k // 4) * 64 + 64]
            h0, l0 = split(part * weight_ref[2 * k : 2 * k + 1, :])
            h1, l1 = split(part * weight_ref[2 * k + 1 : 2 * k + 2, :])
            lhs = jnp.concatenate([h0, l0, h1, l1], axis=0)
            res = dot(lhs, value_ref[:, k * 128 : (k + 1) * 128], 1, 0)
            pair = jnp.where(first, res[0:64] + res[64:128], res[128:192] + res[192:256])
            lanes = slice((k % 2) * 128, (k % 2) * 128 + 128)
            out_ref[k // 2, base : base + 64, lanes] = pair

    one(b_ref[...], wt_ref, x_ref, 0)
    one(c_ref[...], et_ref, dy_ref, 64)
    one(yc_ref[...], yet_ref, ydy_ref, 128)
    out_ref[:, 192:200, :] = row_ref[...]


def summaries(x, dy, b, c, wt, et, ydy, yc, yet, rows):
    length, width = x.shape
    ylen = ydy.shape[0]
    steps = width // 1024

    def cols(n, w):
        return pl.BlockSpec((n, w), lambda i: (0, i))

    def heads(n):
        return pl.BlockSpec((16, n), lambda i: (i, 0))

    return pl.pallas_call(
        summary_kernel,
        grid=(steps,),
        out_shape=jax.ShapeDtypeStruct((16, ROWS, 256), F32),
        in_specs=[
            cols(length, 1024),
            cols(length, 1024),
            cols(length, 128),
            cols(length, 128),
            heads(length),
            heads(length),
            cols(ylen, 1024),
            cols(ylen, 128),
            heads(ylen),
            pl.BlockSpec((4, 8, 256), lambda i: (i, 0, 0)),
        ],
        out_specs=pl.BlockSpec((4, ROWS, 256), lambda i: (i, 0, 0)),
        compiler_params=pltpu.CompilerParams(vmem_limit_bytes=40 * 2**20),
        name="summaries",
    )(x, dy, b, c, wt, et, ydy, yc, yet, rows)


def forward_kernel(core_ref, got_ref, init_ref, end_ref, keep_ref, send_ref):
    core = core_ref[0].astype(F32)
    state = jnp.zeros((64, 256), F32)
    for i in range(16):
        init_ref[i] = state
        state = got_ref[i, 192:193, :] * state + got_ref[i, 0:64, :]
    end_ref[...] = state
    for z in range(4):
        keep = jnp.zeros((64, 256), F32)
        send = jnp.zeros((64, 256), F32)
        for i in range(16):
            owner = got_ref[i, 193:194, :] - 2.0 * z
            term = got_ref[i, 128:192, :]
            keep = keep + jnp.where(owner == core, term, 0.0)
            send = send + jnp.where(owner == 1.0 - core, term, 0.0)
        keep_ref[z] = keep
        send_ref[z] = send


def forward(core, got):
    full = lambda *s: jax.ShapeDtypeStruct(s, F32)
    return pl.pallas_call(
        forward_kernel,
        out_shape=(full(16, 64, 256), full(64, 256), full(4, 64, 256), full(4, 64, 256)),
        in_specs=[pl.BlockSpec(memory_space=pltpu.SMEM), pl.BlockSpec(memory_space=pltpu.VMEM)],
        out_specs=(pl.BlockSpec(memory_space=pltpu.VMEM),) * 4,
        compiler_params=pltpu.CompilerParams(vmem_limit_bytes=40 * 2**20),
        name="forward_scan",
    )(core, got)


def pack_kernel(place_ref, end_ref, keep_ref, recv_ref, m1_ref, m2_ref, m3_ref, own_ref):
    z = place_ref[0]
    own_ref[...] = keep_ref[z] + recv_ref[z]
    for d, ref in ((1, m1_ref), (2, m2_ref), (3, m3_ref)):
        to = lax.rem(z + d, 4)
        ref[0:64] = end_ref[...]
        ref[64:128] = keep_ref[to] + recv_ref[to]


def pack(place, end, keep, recv):
    vmem = pl.BlockSpec(memory_space=pltpu.VMEM)
    msg = jax.ShapeDtypeStruct((128, 256), F32)
    return pl.pallas_call(
        pack_kernel,
        out_shape=(msg, msg, msg, jax.ShapeDtypeStruct((64, 256), F32)),
        in_specs=[pl.BlockSpec(memory_space=pltpu.SMEM)] + [vmem] * 3,
        out_specs=(vmem,) * 4,
        name="pack_leaf",
    )(place, end, keep, recv)


def backward_kernel(
    place_ref, got_ref, init_ref, end_ref, own_ref, r1, r2, r3, s0, s1, s2, s3, out_ref
):
    z = place_ref[0]
    core = place_ref[1]
    grad = own_ref[...] + r1[64:128] + r2[64:128] + r3[64:128]
    for i in range(15, -1, -1):
        out_ref[i, 64:128, :] = grad
        grad = got_ref[i, 192:193, :] * grad + got_ref[i, 64:128, :]
    mine = (end_ref, r1, r2, r3)
    theirs = (s0, s1, s2, s3)
    for i in range(16):
        out_ref[i, 0:64, :] = init_ref[i]
        owner = got_ref[i, 193:194, :]
        start = jnp.zeros((64, 256), F32)
        for d in range(4):
            place = 2 * lax.rem(z + 4 - d, 4)
            here = (place + core).astype(F32)
            there = (place + 1 - core).astype(F32)
            start = start + jnp.where(owner == here, mine[d][0:64], 0.0)
            start = start + jnp.where(owner == there, theirs[d][0:64], 0.0)
        out_ref[i, 128:192, :] = start


def backward(place, got, init, end, own, received, swapped):
    vmem = pl.BlockSpec(memory_space=pltpu.VMEM)
    return pl.pallas_call(
        backward_kernel,
        out_shape=jax.ShapeDtypeStruct((16, 192, 256), F32),
        in_specs=[pl.BlockSpec(memory_space=pltpu.SMEM)] + [vmem] * 11,
        out_specs=vmem,
        compiler_params=pltpu.CompilerParams(vmem_limit_bytes=40 * 2**20),
        name="backward_scan",
    )(place, got, init, end, own, *received, *swapped)


def gradient_kernel(
    chunks,
    init_at,
    grad_at,
    x_ref,
    dy_ref,
    b_ref,
    c_ref,
    cum_ref,
    rate_ref,
    cumt_ref,
    last_ref,
    state_ref,
    dx_ref,
    db_ref,
    dc_ref,
    xh,
    xl,
    yh,
    yl,
    weight,
    carry,
    dci,
    dbo,
    dco,
):
    first = halves(CH)
    causal = lax.broadcasted_iota(jnp.int32, (CH, CH), 1) >= lax.broadcasted_iota(
        jnp.int32, (CH, CH), 0
    )

    def spread(ref, rows, head):
        return jnp.broadcast_to(ref[0, rows, head : head + 1], (CH, 128))

    for g in range(2):
        gcol = g * 512
        pcol = slice(g * 64, g * 64 + 64)

        def start_state(base):
            return jnp.concatenate(
                [state_ref[2 * g, base : base + 64, :], state_ref[2 * g + 1, base : base + 64, :]],
                axis=1,
            )

        def ahead(c, state):
            rows = pl.ds(pl.multiple_of(c * CH, CH), CH)
            for k in range(4):
                head = g * 8 + 2 * k
                lanes = slice(gcol + k * 128, gcol + k * 128 + 128)
                here = slice(k * 128, k * 128 + 128)
                cum = jnp.where(first, spread(cum_ref, rows, head), spread(cum_ref, rows, head + 1))
                rate = jnp.where(
                    first, spread(rate_ref, rows, head), spread(rate_ref, rows, head + 1)
                )
                w = rate * jnp.exp2(last_ref[c, :, lanes] - cum)
                weight[c, :, here] = w
                hi, lo = split(w * x_ref[rows, lanes].astype(F32))
                xh[c, :, here] = hi
                xl[c, :, here] = lo
                hi, lo = split(jnp.exp2(cum) * dy_ref[rows, lanes].astype(F32))
                yh[c, :, here] = hi
                yl[c, :, here] = lo
            b_one = b_ref[rows, pcol]
            c_one = c_ref[rows, pcol]
            added = dot(b_one, xh[c], 0, 0) + dot(b_one, xl[c], 0, 0)
            carry[c] = dot(c_one, yh[c], 0, 0) + dot(c_one, yl[c], 0, 0)
            hi, lo = split(state)
            res = dot(yh[c], jnp.concatenate([hi, lo], axis=0), 1, 1)
            dci[c] = res[:, 0:64] + res[:, 64:128] + dot(yl[c], hi, 1, 1)
            return jnp.exp2(last_ref[c, :, gcol : gcol + 512]) * state + added

        lax.fori_loop(0, chunks, ahead, start_state(init_at))

        def back(step, grad):
            c = chunks - 1 - step
            rows = pl.ds(pl.multiple_of(c * CH, CH), CH)
            b_one = b_ref[rows, pcol]
            c_one = c_ref[rows, pcol]
            ghi, glo = split(grad)
            both = jnp.concatenate([ghi, glo], axis=0)
            dxi = dot(jnp.concatenate([b_one, b_one], axis=1), both, 1, 0) * weight[c]
            res = dot(xh[c], both, 1, 1)
            db = res[:, 0:64] + res[:, 64:128] + dot(xl[c], ghi, 1, 1)
            scores = dot(b_one, c_one, 1, 1)
            total = jnp.zeros((CH, CH), F32)
            for k in range(4):
                lanes = slice(gcol + k * 128, gcol + k * 128 + 128)
                dy = dy_ref[rows, lanes]
                zero = jnp.zeros_like(dy)
                stacked = jnp.concatenate(
                    [jnp.where(first, dy, zero), jnp.where(first, zero, dy)], axis=0
                )
                pairs = dot(x_ref[rows, lanes], stacked, 1, 1)
                his, los = [], []
                for e in range(2):
                    head = g * 8 + 2 * k + e
                    cum_t = cumt_ref[0, c, head : head + 1, :]
                    gap = jnp.where(causal, cum_t - spread(cum_ref, rows, head), -jnp.inf)
                    decay = jnp.exp2(gap) * spread(rate_ref, rows, head)
                    total = total + decay * pairs[:, e * 128 : e * 128 + 128]
                    hi, lo = split(decay * scores)
                    his.append(hi)
                    los.append(lo)
                lhs = jnp.concatenate(
                    [jnp.concatenate(his, axis=1), jnp.concatenate(los, axis=1)], axis=0
                )
                res = dot(lhs, stacked, 1, 0)
                dx = res[0:CH] + res[CH : 2 * CH] + dxi[:, k * 128 : k * 128 + 128]
                dx_ref[rows, lanes] = dx.astype(BF16)
            hi, lo = split(total)
            db = db + dot(hi, c_one, 1, 0) + dot(lo, c_one, 1, 0)
            dc = dci[c] + dot(hi, b_one, 0, 0) + dot(lo, b_one, 0, 0)
            dbo[g, rows, :] = db
            dco[g, rows, :] = dc
            return jnp.exp2(last_ref[c, :, gcol : gcol + 512]) * grad + carry[c]

        if grad_at is None:
            grad = jnp.zeros((64, 512), F32)
        else:
            grad = start_state(grad_at)
        lax.fori_loop(0, chunks, back, grad)
    db_ref[...] = jnp.concatenate([dbo[0], dbo[1]], axis=1).astype(BF16)
    dc_ref[...] = jnp.concatenate([dco[0], dco[1]], axis=1).astype(BF16)


def gradients(x, dy, b, c, cum, rate, cumt, last, states, init_at, grad_at, name):
    length, width = x.shape
    chunks = length // CH
    steps = width // 1024

    def cols(w):
        return pl.BlockSpec((length, w), lambda i: (0, i))

    def scratch(*shape, dtype=F32):
        return pltpu.VMEM(shape, dtype)

    return pl.pallas_call(
        functools.partial(gradient_kernel, chunks, init_at, grad_at),
        grid=(steps,),
        out_shape=(
            jax.ShapeDtypeStruct(x.shape, BF16),
            jax.ShapeDtypeStruct(b.shape, BF16),
            jax.ShapeDtypeStruct(c.shape, BF16),
        ),
        in_specs=[
            cols(1024),
            cols(1024),
            cols(128),
            cols(128),
            pl.BlockSpec((1, length, 16), lambda i: (i, 0, 0)),
            pl.BlockSpec((1, length, 16), lambda i: (i, 0, 0)),
            pl.BlockSpec((1, chunks, 16, CH), lambda i: (i, 0, 0, 0)),
            pl.BlockSpec((chunks, 1, 1024), lambda i: (0, 0, i)),
            pl.BlockSpec((4, 192, 256), lambda i: (i, 0, 0)),
        ],
        out_specs=(cols(1024), cols(128), cols(128)),
        scratch_shapes=[
            scratch(chunks, CH, 512, dtype=BF16),
            scratch(chunks, CH, 512, dtype=BF16),
            scratch(chunks, CH, 512, dtype=BF16),
            scratch(chunks, CH, 512, dtype=BF16),
            scratch(chunks, CH, 512),
            scratch(chunks, 64, 512),
            scratch(chunks, CH, 64),
            scratch(2, length, 64),
            scratch(2, length, 64),
        ],
        compiler_params=pltpu.CompilerParams(vmem_limit_bytes=48 * 2**20),
        name=name,
    )(x, dy, b, c, cum, rate, cumt, last, states)


def rates(step_rates, head_rate):
    length, heads = step_rates.shape
    chunks = length // CH
    logs = (-step_rates * head_rate[None, :]) * LOG2E
    lower = jnp.tril(jnp.ones((CH, CH), F32))
    cum = jnp.einsum("ts,csh->cth", lower, logs.reshape(chunks, CH, heads), precision=HIGHEST)
    last = cum[:, -1]
    by_step = lambda a: a.reshape(length, heads // 16, 16).transpose(1, 0, 2)
    cumt = cum.transpose(0, 2, 1)
    ends = jnp.cumsum(last, axis=0)
    whole = (cumt + (ends - last)[:, :, None]).transpose(1, 0, 2).reshape(heads, length)
    return dict(
        cum=by_step(cum.reshape(length, heads)),
        rate=by_step(step_rates),
        cumt=cumt.reshape(chunks, heads // 16, 16, CH).transpose(1, 0, 2, 3),
        last=jnp.repeat(last, P_SIZE, axis=1)[:, None, :],
        whole=whole,
        end=ends[-1],
    )


def local(
    prompt_x,
    prompt_dt,
    head_rate,
    prompt_b,
    prompt_c,
    prompt_dy,
    branch_x,
    branch_dt,
    branch_b,
    branch_c,
    branch_dy,
    parent,
    lengths,
):
    leaf = lax.axis_index("leaf")
    z, core = leaf // 2, leaf % 2
    place = jnp.stack([z, core]).astype(jnp.int32)
    slots = branch_x.shape[1]
    live = jnp.arange(slots) < lengths[0]
    branch_rates = branch_dt[0] * live[:, None].astype(F32)
    branch_grad = jnp.where(live[:, None], branch_dy[0], jnp.zeros((), BF16))
    pr = rates(prompt_dt[0], head_rate)
    br = rates(branch_rates, head_rate)
    wt = prompt_dt[0].T * jnp.exp2(pr["end"][:, None] - pr["whole"])
    rows = jnp.concatenate(
        [
            jnp.repeat(jnp.exp2(pr["end"]), P_SIZE).reshape(16, 1, 256),
            jnp.broadcast_to(parent[0].astype(F32), (16, 7, 256)),
        ],
        axis=1,
    )
    sent = summaries(
        prompt_x[0],
        prompt_dy[0],
        prompt_b[0],
        prompt_c[0],
        wt,
        jnp.exp2(pr["whole"]),
        branch_grad,
        branch_c[0],
        jnp.exp2(br["whole"]),
        rows,
    )
    got = lax.all_to_all(sent, "seq", 0, 0, tiled=True)
    init, end, keep, send = forward(place[1:], got)
    swap = [(s, s ^ 1) for s in range(8)]
    recv = lax.ppermute(send, "leaf", swap)
    m1, m2, m3, own = pack(place, end, keep, recv)
    received = [
        lax.ppermute(m, "leaf", [(s, (s + 2 * d) % 8) for s in range(8)])
        for d, m in ((1, m1), (2, m2), (3, m3))
    ]
    swapped = [lax.ppermute(m, "leaf", swap) for m in [end] + [m[0:64] for m in received]]
    back = backward(place, got, init, end, own, received, swapped)
    states = lax.all_to_all(back, "seq", 0, 0, tiled=True)
    py = gradients(
        prompt_x[0],
        prompt_dy[0],
        prompt_b[0],
        prompt_c[0],
        pr["cum"],
        pr["rate"],
        pr["cumt"],
        pr["last"],
        states,
        0,
        64,
        "prompt_gradients",
    )
    by = gradients(
        branch_x[0],
        branch_grad,
        branch_b[0],
        branch_c[0],
        br["cum"],
        br["rate"],
        br["cumt"],
        br["last"],
        states,
        128,
        None,
        "branch_gradients",
    )
    return tuple(a[None] for a in py + by)


def solution(mesh):
    seq = P("leaf", "seq", None)
    own = P(("seq", "leaf"), None, None)
    ids = P(("seq", "leaf"))
    in_specs = (seq, seq, P(), seq, seq, seq, own, own, own, own, own, ids, ids)
    out_specs = (seq, seq, seq, own, own, own)
    return jax.shard_map(local, mesh=mesh, in_specs=in_specs, out_specs=out_specs, check_vma=False)
```

```python
import functools
import math

import jax
import jax.numpy as jnp
from jax import lax
from jax.experimental import pallas as pl
from jax.experimental.pallas import tpu as pltpu
from jax.sharding import PartitionSpec as P

P_SIZE = 64
N = 64
CH = 128
LOG2E = math.log2(math.e)
F32 = jnp.float32
BF16 = jnp.bfloat16
BIG = 56
MOST = 56
VMEM = pl.BlockSpec(memory_space=pltpu.VMEM)
SMEM = pl.BlockSpec(memory_space=pltpu.SMEM)


def split(value):
    hi = value.astype(BF16)
    return hi, (value - hi.astype(F32)).astype(BF16)


def dot(a, b, ca, cb):
    return lax.dot_general(a, b, (((ca,), (cb,)), ((), ())), preferred_element_type=F32)


def halves(rows):
    return lax.broadcasted_iota(jnp.int32, (rows, 128), 1) < 64


def cost(micros):
    return pl.CostEstimate(flops=0, bytes_accessed=int(micros * 3.69e6), transcendentals=0)


def limits(mib):
    return pltpu.CompilerParams(vmem_limit_bytes=mib * 2**20)


def call(kernel, in_specs, out_specs, out_shape, args, after=(), **options):
    count, extra = len(args), len(after)

    def body(*refs):
        inner = refs[:count] + refs[count + extra :]
        at = count + len(out_shape)
        inner[at][...] = jnp.zeros((8, 128), F32)
        kernel(*inner[:at], *inner[at + 1 :])

    if "grid" in options:
        token = pl.BlockSpec((8, 128), lambda i: (0, 0))
    else:
        token = VMEM
    return pl.pallas_call(
        body,
        in_specs=in_specs + [pl.BlockSpec(memory_space=pl.ANY)] * extra,
        out_specs=(*out_specs, token),
        out_shape=(*out_shape, jax.ShapeDtypeStruct((8, 128), F32)),
        **options,
    )(*args, *after)


def decay_rates(rate_ref, step):
    head = lax.broadcasted_iota(jnp.int32, (16, 1), 0)
    column = jnp.zeros((16, 1), F32)
    for h in range(16):
        column = jnp.where(head == h, rate_ref[step * 16 + h], column)
    return column * LOG2E


def masked_steps(step_ref, length_ref):
    steps = step_ref[...]
    if length_ref is None:
        return steps, None
    live = lax.broadcasted_iota(jnp.int32, steps.shape, 1) < length_ref[0]
    return jnp.where(live, steps, 0.0), live


def sums(logs, whole):
    row = lax.broadcasted_iota(jnp.int32, (CH, 2 * CH), 0)
    col = lax.broadcasted_iota(jnp.int32, (CH, 2 * CH), 1)
    ones = jnp.where((row <= col) & (col < CH) | (row > col - CH) & (col >= CH), 1.0, 0.0).astype(BF16)
    heads = logs.shape[0]
    chunks = logs.shape[1] // CH
    upto, after, lasts = [], [], []
    for c in range(chunks):
        part = logs[:, c * CH : (c + 1) * CH]
        p1 = part.astype(BF16)
        rest = part - p1.astype(F32)
        p2 = rest.astype(BF16)
        p3 = (rest - p2.astype(F32)).astype(BF16)
        res = dot(jnp.concatenate([p1, p2, p3], axis=0), ones, 1, 0)
        res = res[0:heads] + res[heads : 2 * heads] + res[2 * heads : 3 * heads]
        upto.append(res[:, 0:CH])
        after.append(res[:, CH:])
        lasts.append(res[:, CH - 1 : CH])
    if whole:
        total = jnp.zeros((heads, 1), F32)
        for c in range(chunks):
            upto[c] = upto[c] + total
            total = total + lasts[c]
        total = jnp.zeros((heads, 1), F32)
        for c in range(chunks - 1, -1, -1):
            after[c] = after[c] + total
            total = total + lasts[c]
    return upto, after, lasts


def widen(small):
    row = lax.broadcasted_iota(jnp.int32, (32, 1024), 0)
    lane = lax.broadcasted_iota(jnp.int32, (32, 1024), 1)
    pick = jnp.where(lane // 64 == row % 16, 1.0, 0.0).astype(BF16)
    hi, lo = split(small)
    return dot(jnp.concatenate([hi, lo], axis=0), pick, 0, 0)


def summary(proj_ref, weight, value_ref, out_ref, base):
    first = halves(64)
    proj_t = proj_ref[...].astype(F32).T
    for k in range(8):
        part = proj_t[(k // 4) * 64 : (k // 4) * 64 + 64]
        h0, l0 = split(part * weight[2 * k : 2 * k + 1, :])
        h1, l1 = split(part * weight[2 * k + 1 : 2 * k + 2, :])
        lhs = jnp.concatenate([h0, l0, h1, l1], axis=0)
        res = dot(lhs, value_ref[:, k * 128 : (k + 1) * 128], 1, 0)
        pair = jnp.where(first, res[0:64] + res[64:128], res[128:192] + res[192:256])
        lanes = slice((k % 2) * 128, (k % 2) * 128 + 128)
        out_ref[k // 2, base : base + 64, lanes] = pair


def first_kernel(len_ref, par_ref, rate_ref, x_ref, b_ref, dt_ref, ydy_ref, yc_ref, ydt_ref, out_ref):
    rate = decay_rates(rate_ref, pl.program_id(0))
    steps = dt_ref[...]
    _, after, lasts = sums(-steps * rate, True)
    summary(b_ref, steps * jnp.exp2(jnp.concatenate(after, axis=1)), x_ref, out_ref, 0)
    ysteps, live = masked_steps(ydt_ref, len_ref)
    upto, _, _ = sums(-ysteps * rate, True)
    weight = jnp.where(live, jnp.exp2(jnp.concatenate(upto, axis=1)), 0.0)
    summary(yc_ref, weight, ydy_ref, out_ref, 64)
    decay = jnp.exp2(jnp.broadcast_to(sum(lasts), (16, 256)))
    parent = jnp.zeros((4, 256), F32) + par_ref[0].astype(F32)
    for q in range(4):
        out_ref[q, 128:132, :] = decay[4 * q : 4 * q + 4]
        out_ref[q, 132:136, :] = parent


def carry_kernel(rate_ref, dy_ref, c_ref, dt_ref, out_ref):
    upto, _, _ = sums(-dt_ref[...] * decay_rates(rate_ref, pl.program_id(0)), True)
    summary(c_ref, jnp.exp2(jnp.concatenate(upto, axis=1)), dy_ref, out_ref, 0)


def cols(n, w):
    return pl.BlockSpec((n, w), lambda i: (0, i))


def heads(n):
    return pl.BlockSpec((16, n), lambda i: (i, 0))


def first_message(length, parent, rate, x, b, dt, ydy, yc, ydt):
    n, m = x.shape[0], ydy.shape[0]
    return call(
        first_kernel,
        [SMEM, SMEM, SMEM, cols(n, 1024), cols(n, 128), heads(n)]
        + [cols(m, 1024), cols(m, 128), heads(m)],
        (pl.BlockSpec((4, 136, 256), lambda i: (i, 0, 0)),),
        (jax.ShapeDtypeStruct((16, 136, 256), F32),),
        (length, parent, rate, x, b, dt, ydy, yc, ydt),
        grid=(4,),
        compiler_params=limits(BIG),
        cost_estimate=cost(8),
        name="first_message",
    )


def carry_message(rate, dy, c, dt, after):
    n = dy.shape[0]
    return call(
        carry_kernel,
        [SMEM, cols(n, 1024), cols(n, 128), heads(n)],
        (pl.BlockSpec((4, 64, 256), lambda i: (i, 0, 0)),),
        (jax.ShapeDtypeStruct((16, 64, 256), F32),),
        (rate, dy, c, dt),
        after,
        grid=(4,),
        compiler_params=limits(MOST),
        cost_estimate=cost(6),
        name="carry_message",
    )


def decay_row(got_ref, i):
    lane = lax.broadcasted_iota(jnp.int32, (1, 256), 1)
    row = [got_ref[i, 128 + q : 129 + q, :] for q in range(4)]
    low = jnp.where(lane < 64, row[0], row[1])
    return jnp.where(lane < 128, low, jnp.where(lane < 192, row[2], row[3]))


def forward_kernel(got_ref, carry_ref, out_ref, end_ref):
    state = jnp.zeros((64, 256), F32)
    for i in range(16):
        out_ref[i, 0:64, :] = carry_ref[i]
        out_ref[i, 64:128, :] = state
        state = decay_row(got_ref, i) * state + got_ref[i, 0:64, :]
    end_ref[...] = state


def forward(got, carry, after):
    return call(
        forward_kernel,
        [VMEM] * 2,
        (VMEM,) * 2,
        (jax.ShapeDtypeStruct((16, 128, 256), F32), jax.ShapeDtypeStruct((64, 256), F32)),
        (got, carry),
        after,
        compiler_params=limits(BIG),
        cost_estimate=cost(1),
        name="forward_scan",
    )


def buckets_kernel(place_ref, got_ref, end_ref, keep_ref, send_ref):
    core = place_ref[1].astype(F32)
    send_ref[4] = end_ref[...]
    for z in range(4):
        keep = jnp.zeros((64, 256), F32)
        send = jnp.zeros((64, 256), F32)
        for i in range(16):
            owner = got_ref[i, 132:133, :] - 2.0 * z
            term = got_ref[i, 64:128, :]
            keep = keep + jnp.where(owner == core, term, 0.0)
            send = send + jnp.where(owner == 1.0 - core, term, 0.0)
        keep_ref[z] = keep
        send_ref[z] = send


def buckets(place, got, end):
    return call(
        buckets_kernel,
        [SMEM, VMEM, VMEM],
        (VMEM,) * 2,
        (jax.ShapeDtypeStruct((4, 64, 256), F32), jax.ShapeDtypeStruct((5, 64, 256), F32)),
        (place, got, end),
        compiler_params=limits(BIG),
        cost_estimate=cost(1),
        name="buckets",
    )


def pack_kernel(place_ref, end_ref, keep_ref, recv_ref, m1_ref, m2_ref, m3_ref, own_ref):
    z = place_ref[0]
    own_ref[...] = keep_ref[z] + recv_ref[z]
    for d, ref in ((1, m1_ref), (2, m2_ref), (3, m3_ref)):
        to = lax.rem(z + d, 4)
        ref[0] = end_ref[...]
        ref[1] = recv_ref[4]
        ref[2] = keep_ref[to] + recv_ref[to]


def pack(place, end, keep, recv):
    msg = jax.ShapeDtypeStruct((3, 64, 256), F32)
    return call(
        pack_kernel,
        [SMEM] + [VMEM] * 3,
        (VMEM,) * 4,
        (msg, msg, msg, jax.ShapeDtypeStruct((64, 256), F32)),
        (place, end, keep, recv),
        compiler_params=limits(BIG),
        cost_estimate=cost(1),
        name="pack_leaf",
    )


def backward_kernel(got_ref, carry_ref, own_ref, r1, r2, r3, grad_ref):
    grad = own_ref[...] + r1[2] + r2[2] + r3[2]
    for i in range(15, -1, -1):
        grad_ref[i] = grad
        grad = decay_row(got_ref, i) * grad + carry_ref[i, 0:64, :]


def starts_kernel(place_ref, gotb_ref, end_ref, recv_ref, r1, r2, r3, start_ref):
    z = place_ref[0]
    core = place_ref[1]
    mine = (end_ref[...], r1[0], r2[0], r3[0])
    theirs = (recv_ref[4], r1[1], r2[1], r3[1])
    for i in range(16):
        owner = gotb_ref[i, 132:133, :]
        start = jnp.zeros((64, 256), F32)
        for d in range(4):
            place = 2 * lax.rem(z + 4 - d, 4)
            here = (place + core).astype(F32)
            there = (place + 1 - core).astype(F32)
            start = start + jnp.where(owner == here, mine[d], 0.0)
            start = start + jnp.where(owner == there, theirs[d], 0.0)
        start_ref[i] = start


def states_back(kernel, scalars, args, after, name):
    return call(
        kernel,
        [SMEM] * len(scalars) + [VMEM] * len(args),
        (VMEM,),
        (jax.ShapeDtypeStruct((16, 64, 256), F32),),
        (*scalars, *args),
        after,
        compiler_params=limits(BIG),
        cost_estimate=cost(1.5),
        name=name,
    )


def inside_kernel(chunks, has_length, *refs):
    step = pl.program_id(0)
    if has_length:
        len_ref, refs = refs[0], refs[1:]
    else:
        len_ref = None
    rate_ref, x_ref, dy_ref, b_ref, c_ref, dt_ref, dx_ref, db_ref, dc_ref = refs[:9]
    xh, xl, yh, yl, weight = refs[9:]
    first = halves(CH)
    causal = lax.broadcasted_iota(jnp.int32, (CH, CH), 1) >= lax.broadcasted_iota(
        jnp.int32, (CH, CH), 0
    )
    steps, _ = masked_steps(dt_ref, len_ref)
    upto, after, _ = sums(-steps * decay_rates(rate_ref, step), False)
    state = [jnp.zeros((64, 512), F32)] * 2
    carry, ends, dci = {}, {}, {}

    def grads_out(c):
        dy = dy_ref[c * CH : (c + 1) * CH, :]
        if len_ref is None:
            return dy
        token = lax.broadcasted_iota(jnp.int32, (CH, 1024), 0) + c * CH
        return jnp.where(token < len_ref[0], dy.astype(F32), 0.0).astype(BF16)

    def cross(lhs_hi, lhs_lo, rhs):
        hi, lo = split(rhs)
        res = dot(lhs_hi, jnp.concatenate([hi, lo], axis=0), 1, 1)
        return res[:, 0:64] + res[:, 64:128] + dot(lhs_lo, hi, 1, 1)

    for c in range(chunks):
        rows = slice(c * CH, (c + 1) * CH)
        rate_c = steps[:, rows]
        w = widen(rate_c * jnp.exp2(after[c]))
        e = widen(jnp.exp2(upto[c]))
        ends[c] = e[CH - 1 : CH]
        weight[c] = w
        xh[c], xl[c] = split(w * x_ref[rows, :].astype(F32))
        yh[c], yl[c] = split(e * grads_out(c).astype(F32))
        for g in range(2):
            wide = slice(g * 512, g * 512 + 512)
            thin = slice(g * 64, g * 64 + 64)
            if c > 0:
                dci[c, g] = cross(yh[c, :, wide], yl[c, :, wide], state[g])
            if c < chunks - 1:
                b_one = b_ref[rows, thin]
                added = dot(b_one, xh[c, :, wide], 0, 0) + dot(b_one, xl[c, :, wide], 0, 0)
                state[g] = added if c == 0 else ends[c][:, wide] * state[g] + added
            if c > 0:
                c_one = c_ref[rows, thin]
                carry[c, g] = dot(c_one, yh[c, :, wide], 0, 0) + dot(c_one, yl[c, :, wide], 0, 0)
    grad = [None, None]
    for c in range(chunks - 1, -1, -1):
        rows = slice(c * CH, (c + 1) * CH)
        cum_t = upto[c]
        cum_s = cum_t.T
        rate_s = steps[:, rows].T
        dy_c = grads_out(c)
        for g in range(2):
            wide = slice(g * 512, g * 512 + 512)
            thin = slice(g * 64, g * 64 + 64)
            b_one = b_ref[rows, thin]
            c_one = c_ref[rows, thin]
            dxi = None
            if c < chunks - 1:
                hi, lo = split(grad[g])
                dxi = dot(
                    jnp.concatenate([b_one, b_one], axis=1),
                    jnp.concatenate([hi, lo], axis=0),
                    1,
                    0,
                )
                dxi = dxi * weight[c, :, wide]
                dbi = cross(xh[c, :, wide], xl[c, :, wide], grad[g])
            scores = dot(b_one, c_one, 1, 1)
            total = jnp.zeros((CH, CH), F32)
            for k in range(4):
                lanes = slice(g * 512 + k * 128, g * 512 + k * 128 + 128)
                dy = dy_c[:, lanes]
                zero = jnp.zeros_like(dy)
                stacked = jnp.concatenate(
                    [jnp.where(first, dy, zero), jnp.where(first, zero, dy)], axis=0
                )
                pairs = dot(x_ref[rows, lanes], stacked, 1, 1)
                his, los = [], []
                for e in range(2):
                    h = g * 8 + 2 * k + e
                    gap = cum_t[h : h + 1, :] - jnp.broadcast_to(cum_s[:, h : h + 1], (CH, CH))
                    decay = jnp.exp2(jnp.where(causal, gap, -jnp.inf))
                    decay = decay * jnp.broadcast_to(rate_s[:, h : h + 1], (CH, CH))
                    total = total + decay * pairs[:, e * CH : (e + 1) * CH]
                    hi, lo = split(decay * scores)
                    his.append(hi)
                    los.append(lo)
                lhs = jnp.concatenate(
                    [jnp.concatenate(his, axis=1), jnp.concatenate(los, axis=1)], axis=0
                )
                res = dot(lhs, stacked, 1, 0)
                dx = res[0:CH] + res[CH : 2 * CH]
                if dxi is not None:
                    dx = dx + dxi[:, k * 128 : k * 128 + 128]
                dx_ref[rows, lanes] = dx.astype(dx_ref.dtype)
            hi, lo = split(total)
            db = dot(hi, c_one, 1, 0) + dot(lo, c_one, 1, 0)
            dc = dot(hi, b_one, 0, 0) + dot(lo, b_one, 0, 0)
            if c < chunks - 1:
                db = db + dbi
            if c > 0:
                dc = dc + dci[c, g]
                first_grad = c == chunks - 1
                grad[g] = carry[c, g] if first_grad else ends[c][:, wide] * grad[g] + carry[c, g]
            db_ref[rows, thin] = db.astype(db_ref.dtype)
            dc_ref[rows, thin] = dc


def inside(length, rate, x, dy, b, c, dt, kind, after, micros, name):
    n = x.shape[0]
    chunks = n // CH

    def scratch(dtype):
        return pltpu.VMEM((chunks, CH, 1024), dtype)

    has_length = length is not None
    return call(
        functools.partial(inside_kernel, chunks, has_length),
        [SMEM] * has_length + [SMEM, cols(n, 1024), cols(n, 1024), cols(n, 128), cols(n, 128), heads(n)],
        (cols(n, 1024), cols(n, 128), cols(n, 128)),
        (
            jax.ShapeDtypeStruct(x.shape, kind),
            jax.ShapeDtypeStruct(b.shape, kind),
            jax.ShapeDtypeStruct(c.shape, F32),
        ),
        (*([length] if has_length else []), rate, x, dy, b, c, dt),
        after,
        grid=(4,),
        scratch_shapes=[scratch(BF16)] * 4 + [scratch(F32)],
        compiler_params=limits(MOST),
        cost_estimate=cost(micros),
        name=name,
    )


def state_of(ref, g, base):
    return jnp.concatenate(
        [ref[2 * g, base : base + 64, :], ref[2 * g + 1, base : base + 64, :]], axis=1
    )


def start_kernel(base, has_length, *refs):
    if has_length:
        len_ref, refs = refs[0], refs[1:]
    else:
        len_ref = None
    rate_ref, dy_ref, dt_ref, state_ref, part_ref, dc_ref = refs
    steps, live = masked_steps(dt_ref, len_ref)
    upto, _, _ = sums(-steps * decay_rates(rate_ref, pl.program_id(0)), True)
    weight = jnp.exp2(jnp.concatenate(upto, axis=1))
    if live is not None:
        weight = jnp.where(live, weight, 0.0)
    yh, yl = split(widen(weight) * dy_ref[...].astype(F32))
    out = []
    for g in range(2):
        wide = slice(g * 512, g * 512 + 512)
        hi, lo = split(state_of(state_ref, g, base))
        res = dot(yh[:, wide], jnp.concatenate([hi, lo], axis=0), 1, 1)
        out.append(res[:, 0:64] + res[:, 64:128] + dot(yl[:, wide], hi, 1, 1))
    dc_ref[...] = (part_ref[...] + jnp.concatenate(out, axis=1)).astype(BF16)


def from_start(length, rate, dy, dt, states, base, part, after, name):
    n = dy.shape[0]
    has_length = length is not None
    return call(
        functools.partial(start_kernel, base, has_length),
        [SMEM] * has_length
        + [SMEM, cols(n, 1024), heads(n)]
        + [pl.BlockSpec((4,) + states.shape[1:], lambda i: (i, 0, 0)), cols(n, 128)],
        (cols(n, 128),),
        (jax.ShapeDtypeStruct((n, 512), BF16),),
        (*([length] if has_length else []), rate, dy, dt, states, part),
        after,
        grid=(4,),
        compiler_params=limits(MOST),
        cost_estimate=cost(n / 64),
        name=name,
    )


def end_kernel(base, rate_ref, x_ref, b_ref, dt_ref, state_ref, dxp_ref, dbp_ref, dx_ref, db_ref):
    steps = dt_ref[...]
    _, after, _ = sums(-steps * decay_rates(rate_ref, pl.program_id(0)), True)
    w = widen(steps * jnp.exp2(jnp.concatenate(after, axis=1)))
    xh, xl = split(w * x_ref[...].astype(F32))
    out = []
    for g in range(2):
        wide = slice(g * 512, g * 512 + 512)
        b_one = b_ref[:, g * 64 : g * 64 + 64]
        hi, lo = split(state_of(state_ref, g, base))
        both = jnp.concatenate([hi, lo], axis=0)
        dx = dot(jnp.concatenate([b_one, b_one], axis=1), both, 1, 0) * w[:, wide]
        dx_ref[:, wide] = (dxp_ref[:, wide] + dx).astype(BF16)
        res = dot(xh[:, wide], both, 1, 1)
        out.append(res[:, 0:64] + res[:, 64:128] + dot(xl[:, wide], hi, 1, 1))
    db_ref[...] = (dbp_ref[...] + jnp.concatenate(out, axis=1)).astype(BF16)


def from_end(rate, x, b, dt, states, base, dx_part, db_part):
    n = x.shape[0]
    return call(
        functools.partial(end_kernel, base),
        [SMEM, cols(n, 1024), cols(n, 128), heads(n)]
        + [pl.BlockSpec((4,) + states.shape[1:], lambda i: (i, 0, 0)), cols(n, 1024), cols(n, 128)],
        (cols(n, 1024), cols(n, 128)),
        (jax.ShapeDtypeStruct(x.shape, BF16), jax.ShapeDtypeStruct(b.shape, BF16)),
        (rate, x, b, dt, states, dx_part, db_part),
        grid=(4,),
        compiler_params=limits(MOST),
        cost_estimate=cost(10),
        name="from_end",
    )


def local(
    prompt_x,
    prompt_dt,
    head_rate,
    prompt_b,
    prompt_c,
    prompt_dy,
    branch_x,
    branch_dt,
    branch_b,
    branch_c,
    branch_dy,
    parent,
    lengths,
):
    x, dy, b, c = prompt_x[0], prompt_dy[0], prompt_b[0], prompt_c[0]
    yx, ydy, yb, yc = branch_x[0], branch_dy[0], branch_b[0], branch_c[0]
    dt, ydt = prompt_dt[0].T, branch_dt[0].T
    rate = head_rate
    leaf = lax.axis_index("leaf")
    place = jnp.stack([leaf // 2, leaf % 2]).astype(jnp.int32)
    swap = [(s, s ^ 1) for s in range(8)]

    def turn(value):
        return lax.all_to_all(value, "seq", 0, 0, tiled=True)

    sent, t = first_message(lengths, parent, rate, x, b, dt, ydy, yc, ydt)
    got = turn(sent)
    csent, t = carry_message(rate, dy, c, dt, (t,))
    dx_part, db_part, dc_part, t = inside(
        None, rate, x, dy, b, c, dt, F32, (t,), 28, "prompt_inside"
    )
    second, end, _ = forward(got, csent, (t,))
    back = turn(second)
    keep, send, _ = buckets(place, got, end)
    recv = lax.ppermute(send, "leaf", swap)
    m1, m2, m3, own, t = pack(place, end, keep, recv)
    received = [
        lax.ppermute(m, "leaf", [(s, (s + 2 * d) % 8) for s in range(8)])
        for d, m in ((1, m1), (2, m2), (3, m3))
    ]
    ydx, ydb, ydc_part, t = inside(
        lengths, rate, yx, ydy, yb, yc, ydt, BF16, (t,), 14, "branch_inside"
    )
    grads, t = states_back(
        backward_kernel, (), (got, back, own, *received), (t,), "end_gradients"
    )
    grads = turn(grads)
    dc, t = from_start(None, rate, dy, dt, back, 64, dc_part, (t,), "prompt_from_start")
    starts, t = states_back(
        starts_kernel, (place,), (got, end, recv, *received), (t,), "branch_starts"
    )
    starts = turn(starts)
    dx, db, t = from_end(rate, x, b, dt, grads, 0, dx_part, db_part)
    ydc, _ = from_start(lengths, rate, ydy, ydt, starts, 0, ydc_part, (t,), "branch_from_start")
    return tuple(a[None] for a in (dx, db, dc, ydx, ydb, ydc))


def solution(mesh):
    seq = P("leaf", "seq", None)
    own = P(("seq", "leaf"), None, None)
    ids = P(("seq", "leaf"))
    in_specs = (seq, seq, P(), seq, seq, seq, own, own, own, own, own, ids, ids)
    out_specs = (seq, seq, seq, own, own, own)
    return jax.shard_map(local, mesh=mesh, in_specs=in_specs, out_specs=out_specs, check_vma=False)
```

```python
import functools
import math

import jax
import jax.numpy as jnp
from jax import lax
from jax.experimental import pallas as pl
from jax.experimental.pallas import tpu as pltpu
from jax.sharding import PartitionSpec as P

P_SIZE = 64
N = 64
CH = 128
LOG2E = math.log2(math.e)
F32 = jnp.float32
BF16 = jnp.bfloat16
BIG = 56
MOST = 56
VMEM = pl.BlockSpec(memory_space=pltpu.VMEM)
SMEM = pl.BlockSpec(memory_space=pltpu.SMEM)


def split(value):
    hi = value.astype(BF16)
    return hi, (value - hi.astype(F32)).astype(BF16)


def dot(a, b, ca, cb):
    return lax.dot_general(a, b, (((ca,), (cb,)), ((), ())), preferred_element_type=F32)


def halves(rows):
    return lax.broadcasted_iota(jnp.int32, (rows, 128), 1) < 64


def cost(micros):
    return pl.CostEstimate(flops=0, bytes_accessed=int(micros * 3.69e6), transcendentals=0)


def limits(mib):
    return pltpu.CompilerParams(vmem_limit_bytes=mib * 2**20)


def call(kernel, in_specs, out_specs, out_shape, args, after=(), **options):
    if after:
        *args, _ = lax.optimization_barrier((*args, after))
    return pl.pallas_call(
        kernel, in_specs=in_specs, out_specs=out_specs, out_shape=out_shape, **options
    )(*args)


def masked_steps(step_ref, length_ref):
    steps = step_ref[...]
    if length_ref is None:
        return steps, None
    live = lax.broadcasted_iota(jnp.int32, steps.shape, 1) < length_ref[0]
    return jnp.where(live, steps, 0.0), live


def sums(logs):
    row = lax.broadcasted_iota(jnp.int32, (CH, 2 * CH), 0)
    col = lax.broadcasted_iota(jnp.int32, (CH, 2 * CH), 1)
    ones = jnp.where((row <= col) & (col < CH) | (row > col - CH) & (col >= CH), 1.0, 0.0).astype(BF16)
    count = logs.shape[0]
    chunks = logs.shape[1] // CH
    upto, after, lasts = [], [], []
    for c in range(chunks):
        part = logs[:, c * CH : (c + 1) * CH]
        p1 = part.astype(BF16)
        rest = part - p1.astype(F32)
        p2 = rest.astype(BF16)
        p3 = (rest - p2.astype(F32)).astype(BF16)
        res = dot(jnp.concatenate([p1, p2, p3], axis=0), ones, 1, 0)
        res = res[0:count] + res[count : 2 * count] + res[2 * count : 3 * count]
        upto.append(res[:, 0:CH])
        after.append(res[:, CH:])
        lasts.append(res[:, CH - 1 : CH])
    zero = jnp.zeros((count, 1), F32)
    before, behind = [zero], [zero]
    for c in range(chunks):
        before.append(before[c] + lasts[c])
        behind.append(behind[c] + lasts[chunks - 1 - c])
    return upto, after, before[:chunks], behind[chunks - 1 :: -1] if chunks > 1 else behind[:1], before[chunks]


def picker():
    row = lax.broadcasted_iota(jnp.int32, (32, 1024), 0)
    lane = lax.broadcasted_iota(jnp.int32, (32, 1024), 1)
    return jnp.where(lane // 64 == row % 16, 1.0, 0.0).astype(BF16)


def turned(small):
    hi = small.astype(BF16).astype(F32)
    return jnp.concatenate([hi, small - hi], axis=0).T.astype(BF16)


def summary(proj_ref, weight, value_ref, out_ref, base):
    first = halves(64)
    proj_t = proj_ref[...].astype(F32).T
    for k in range(8):
        part = proj_t[(k // 4) * 64 : (k // 4) * 64 + 64]
        h0, l0 = split(part * weight[2 * k : 2 * k + 1, :])
        h1, l1 = split(part * weight[2 * k + 1 : 2 * k + 2, :])
        lhs = jnp.concatenate([h0, l0, h1, l1], axis=0)
        res = dot(lhs, value_ref[:, k * 128 : (k + 1) * 128], 1, 0)
        pair = jnp.where(first, res[0:64] + res[64:128], res[128:192] + res[192:256])
        lanes = slice((k % 2) * 128, (k % 2) * 128 + 128)
        out_ref[k // 2, base : base + 64, lanes] = pair


def first_kernel(
    len_ref,
    par_ref,
    rate_ref,
    x_ref,
    b_ref,
    dt_ref,
    ydy_ref,
    yc_ref,
    ydt_ref,
    out_ref,
    upto_ref,
    after_ref,
    yupto_ref,
    yafter_ref,
    e_ref,
    w_ref,
    ye_ref,
    w_all,
    e_all,
    ye_all,
    end_all,
):
    step = pl.program_id(0)

    @pl.when(step == 0)
    def _():
        rate = jnp.broadcast_to(rate_ref[...], (CH, 64)).T[:, 0:1] * LOG2E
        steps = dt_ref[...]
        upto, after, before, behind, end = sums(-steps * rate)
        for c in range(len(upto)):
            here = slice(c * CH, (c + 1) * CH)
            upto_ref[:, here] = upto[c]
            after_ref[:, here] = after[c]
            e_all[:, here] = jnp.exp2(upto[c] + before[c])
            w_all[:, here] = steps[:, here] * jnp.exp2(after[c] + behind[c])
        end_all[...] = jnp.exp2(jnp.broadcast_to(end, end_all.shape))
        ysteps, live = masked_steps(ydt_ref, len_ref)
        upto, after, before, _, _ = sums(-ysteps * rate)
        for c in range(len(upto)):
            here = slice(c * CH, (c + 1) * CH)
            yupto_ref[:, here] = upto[c]
            yafter_ref[:, here] = after[c]
            ye_all[:, here] = jnp.where(live[:, here], jnp.exp2(upto[c] + before[c]), 0.0)

    rows = pl.ds(pl.multiple_of(step * 16, 16), 16)
    w, ye = w_all[rows, :], ye_all[rows, :]
    summary(b_ref, w, x_ref, out_ref, 0)
    summary(yc_ref, ye, ydy_ref, out_ref, 64)
    decay = end_all[rows, :]
    parent = jnp.zeros((4, 256), F32) + par_ref[0].astype(F32)
    for q in range(4):
        out_ref[q, 128:132, :] = decay[4 * q : 4 * q + 4]
        out_ref[q, 132:136, :] = parent
    e_ref[0] = turned(e_all[rows, :])
    w_ref[0] = turned(w)
    ye_ref[0] = turned(ye)


def cols(n, w):
    return pl.BlockSpec((n, w), lambda i: (0, i))


def heads(n):
    return pl.BlockSpec((16, n), lambda i: (i, 0))


def whole(*shape):
    return pl.BlockSpec(shape, lambda i: (0,) * len(shape))


def turns(n):
    return pl.BlockSpec((1, n, 32), lambda i: (i, 0, 0))


def first_message(length, parent, rate, x, b, dt, ydy, yc, ydt):
    n, m = x.shape[0], ydy.shape[0]
    f32 = lambda *shape: jax.ShapeDtypeStruct(shape, F32)
    bf16 = lambda *shape: jax.ShapeDtypeStruct(shape, BF16)
    return call(
        first_kernel,
        [SMEM, SMEM, whole(1, 64), cols(n, 1024), cols(n, 128), whole(64, n)]
        + [cols(m, 1024), cols(m, 128), whole(64, m)],
        (pl.BlockSpec((4, 136, 256), lambda i: (i, 0, 0)),)
        + (whole(64, n),) * 2
        + (whole(64, m),) * 2
        + (turns(n), turns(n), turns(m)),
        (f32(16, 136, 256), f32(64, n), f32(64, n), f32(64, m), f32(64, m))
        + (bf16(4, n, 32), bf16(4, n, 32), bf16(4, m, 32)),
        (length, parent, rate, x, b, dt, ydy, yc, ydt),
        grid=(4,),
        scratch_shapes=[
            pltpu.VMEM((64, n), F32),
            pltpu.VMEM((64, n), F32),
            pltpu.VMEM((64, m), F32),
            pltpu.VMEM((64, 256), F32),
        ],
        compiler_params=limits(BIG),
        cost_estimate=cost(8),
        name="first_message",
    )


def decay_row(got_ref, i):
    lane = lax.broadcasted_iota(jnp.int32, (1, 256), 1)
    row = [got_ref[i, 128 + q : 129 + q, :] for q in range(4)]
    low = jnp.where(lane < 64, row[0], row[1])
    return jnp.where(lane < 128, low, jnp.where(lane < 192, row[2], row[3]))


def forward_kernel(got_ref, carry_ref, out_ref, end_ref):
    state = jnp.zeros((64, 256), F32)
    for i in range(16):
        out_ref[i, 0:64, :] = carry_ref[i]
        out_ref[i, 64:128, :] = state
        state = decay_row(got_ref, i) * state + got_ref[i, 0:64, :]
    end_ref[...] = state


def forward(got, carry, after):
    return call(
        forward_kernel,
        [VMEM] * 2,
        (VMEM,) * 2,
        (jax.ShapeDtypeStruct((16, 128, 256), F32), jax.ShapeDtypeStruct((64, 256), F32)),
        (got, carry),
        after,
        compiler_params=limits(12),
        cost_estimate=cost(1),
        name="forward_scan",
    )


def buckets_kernel(place_ref, got_ref, end_ref, keep_ref, send_ref):
    core = place_ref[1].astype(F32)
    send_ref[4] = end_ref[...]
    for z in range(4):
        keep = jnp.zeros((64, 256), F32)
        send = jnp.zeros((64, 256), F32)
        for i in range(16):
            owner = got_ref[i, 132:133, :] - 2.0 * z
            term = got_ref[i, 64:128, :]
            keep = keep + jnp.where(owner == core, term, 0.0)
            send = send + jnp.where(owner == 1.0 - core, term, 0.0)
        keep_ref[z] = keep
        send_ref[z] = send


def buckets(place, got, end):
    return call(
        buckets_kernel,
        [SMEM, VMEM, VMEM],
        (VMEM,) * 2,
        (jax.ShapeDtypeStruct((4, 64, 256), F32), jax.ShapeDtypeStruct((5, 64, 256), F32)),
        (place, got, end),
        compiler_params=limits(12),
        cost_estimate=cost(1),
        name="buckets",
    )


def pack_kernel(place_ref, end_ref, keep_ref, recv_ref, m1_ref, m2_ref, m3_ref, own_ref):
    z = place_ref[0]
    own_ref[...] = keep_ref[z] + recv_ref[z]
    for d, ref in ((1, m1_ref), (2, m2_ref), (3, m3_ref)):
        to = lax.rem(z + d, 4)
        ref[0] = end_ref[...]
        ref[1] = recv_ref[4]
        ref[2] = keep_ref[to] + recv_ref[to]


def pack(place, end, keep, recv):
    msg = jax.ShapeDtypeStruct((3, 64, 256), F32)
    return call(
        pack_kernel,
        [SMEM] + [VMEM] * 3,
        (VMEM,) * 4,
        (msg, msg, msg, jax.ShapeDtypeStruct((64, 256), F32)),
        (place, end, keep, recv),
        compiler_params=limits(12),
        cost_estimate=cost(1),
        name="pack_leaf",
    )


def backward_kernel(got_ref, carry_ref, own_ref, r1, r2, r3, grad_ref):
    grad = own_ref[...] + r1[2] + r2[2] + r3[2]
    for i in range(15, -1, -1):
        grad_ref[i] = grad
        grad = decay_row(got_ref, i) * grad + carry_ref[i, 0:64, :]


def starts_kernel(place_ref, gotb_ref, end_ref, recv_ref, r1, r2, r3, start_ref):
    z = place_ref[0]
    core = place_ref[1]
    mine = (end_ref[...], r1[0], r2[0], r3[0])
    theirs = (recv_ref[4], r1[1], r2[1], r3[1])
    for i in range(16):
        owner = gotb_ref[i, 132:133, :]
        start = jnp.zeros((64, 256), F32)
        for d in range(4):
            place = 2 * lax.rem(z + 4 - d, 4)
            here = (place + core).astype(F32)
            there = (place + 1 - core).astype(F32)
            start = start + jnp.where(owner == here, mine[d], 0.0)
            start = start + jnp.where(owner == there, theirs[d], 0.0)
        start_ref[i] = start


def states_back(kernel, scalars, args, after, name):
    return call(
        kernel,
        [SMEM] * len(scalars) + [VMEM] * len(args),
        (VMEM,),
        (jax.ShapeDtypeStruct((16, 64, 256), F32),),
        (*scalars, *args),
        after,
        compiler_params=limits(12),
        cost_estimate=cost(1.5),
        name=name,
    )


def inside_kernel(chunks, has_length, *refs):
    if has_length:
        len_ref, refs = refs[0], refs[1:]
    else:
        len_ref = None
    x_ref, dy_ref, b_ref, c_ref, dt_ref, upto_ref, after_ref, dx_ref, db_ref, dc_ref = refs[:10]
    if has_length:
        carry_ref = None
        xh, xl, yh, yl, weight = refs[10:]
    else:
        carry_ref = refs[10]
        xh, xl, yh, yl, weight = refs[11:]
    pick = picker()
    first = halves(CH)
    causal = lax.broadcasted_iota(jnp.int32, (CH, CH), 1) >= lax.broadcasted_iota(
        jnp.int32, (CH, CH), 0
    )
    steps, _ = masked_steps(dt_ref, len_ref)
    upto = [upto_ref[:, c * CH : (c + 1) * CH] for c in range(chunks)]
    after = [after_ref[:, c * CH : (c + 1) * CH] for c in range(chunks)]
    state = [jnp.zeros((64, 512), F32)] * 2
    carry, ends, dci = {}, {}, {}

    def grads_out(c):
        dy = dy_ref[c * CH : (c + 1) * CH, :]
        if len_ref is None:
            return dy
        token = lax.broadcasted_iota(jnp.int32, (CH, 1024), 0) + c * CH
        return jnp.where(token < len_ref[0], dy.astype(F32), 0.0).astype(BF16)

    def cross(lhs_hi, lhs_lo, rhs):
        hi, lo = split(rhs)
        res = dot(lhs_hi, jnp.concatenate([hi, lo], axis=0), 1, 1)
        return res[:, 0:64] + res[:, 64:128] + dot(lhs_lo, hi, 1, 1)

    for c in range(chunks):
        rows = slice(c * CH, (c + 1) * CH)
        rate_c = steps[:, rows]
        w_turned = turned(rate_c * jnp.exp2(after[c]))
        e_turned = turned(jnp.exp2(upto[c]))
        dy_c = grads_out(c)
        tails = []
        for q in range(4):
            lanes = slice(q * 256, q * 256 + 256)
            w = dot(w_turned, pick[:, lanes], 1, 0)
            weight[c, :, lanes] = w
            xh[c, :, lanes], xl[c, :, lanes] = split(w * x_ref[rows, lanes].astype(F32))
            e = dot(e_turned, pick[:, lanes], 1, 0)
            tails.append(e[CH - 1 : CH])
            yh[c, :, lanes], yl[c, :, lanes] = split(e * dy_c[:, lanes].astype(F32))
        ends[c] = jnp.concatenate(tails, axis=1)
        for g in range(2):
            wide = slice(g * 512, g * 512 + 512)
            thin = slice(g * 64, g * 64 + 64)
            if c > 0:
                dci[c, g] = cross(yh[c, :, wide], yl[c, :, wide], state[g])
            if c < chunks - 1:
                b_one = b_ref[rows, thin]
                added = dot(b_one, xh[c, :, wide], 0, 0) + dot(b_one, xl[c, :, wide], 0, 0)
                state[g] = added if c == 0 else ends[c][:, wide] * state[g] + added
            if c > 0 or carry_ref is not None:
                c_one = c_ref[rows, thin]
                carry[c, g] = dot(c_one, yh[c, :, wide], 0, 0) + dot(c_one, yl[c, :, wide], 0, 0)
    grad = [None, None]
    for c in range(chunks - 1, -1, -1):
        rows = slice(c * CH, (c + 1) * CH)
        cum_t = upto[c]
        cum_s = cum_t.T
        rate_s = steps[:, rows].T
        dy_c = grads_out(c)
        for g in range(2):
            wide = slice(g * 512, g * 512 + 512)
            thin = slice(g * 64, g * 64 + 64)
            b_one = b_ref[rows, thin]
            c_one = c_ref[rows, thin]
            dxi = None
            if c < chunks - 1:
                hi, lo = split(grad[g])
                dxi = dot(
                    jnp.concatenate([b_one, b_one], axis=1),
                    jnp.concatenate([hi, lo], axis=0),
                    1,
                    0,
                )
                dxi = dxi * weight[c, :, wide]
                dbi = cross(xh[c, :, wide], xl[c, :, wide], grad[g])
            scores = dot(b_one, c_one, 1, 1)
            total = jnp.zeros((CH, CH), F32)
            for k in range(4):
                lanes = slice(g * 512 + k * 128, g * 512 + k * 128 + 128)
                dy = dy_c[:, lanes]
                zero = jnp.zeros_like(dy)
                stacked = jnp.concatenate(
                    [jnp.where(first, dy, zero), jnp.where(first, zero, dy)], axis=0
                )
                pairs = dot(x_ref[rows, lanes], stacked, 1, 1)
                his, los = [], []
                for e in range(2):
                    h = g * 8 + 2 * k + e
                    gap = cum_t[h : h + 1, :] - jnp.broadcast_to(cum_s[:, h : h + 1], (CH, CH))
                    decay = jnp.exp2(jnp.where(causal, gap, -jnp.inf))
                    decay = decay * jnp.broadcast_to(rate_s[:, h : h + 1], (CH, CH))
                    total = total + decay * pairs[:, e * CH : (e + 1) * CH]
                    hi, lo = split(decay * scores)
                    his.append(hi)
                    los.append(lo)
                lhs = jnp.concatenate(
                    [jnp.concatenate(his, axis=1), jnp.concatenate(los, axis=1)], axis=0
                )
                res = dot(lhs, stacked, 1, 0)
                dx = res[0:CH] + res[CH : 2 * CH]
                if dxi is not None:
                    dx = dx + dxi[:, k * 128 : k * 128 + 128]
                dx_ref[rows, lanes] = dx.astype(dx_ref.dtype)
            hi, lo = split(total)
            db = dot(hi, c_one, 1, 0) + dot(lo, c_one, 1, 0)
            dc = dot(hi, b_one, 0, 0) + dot(lo, b_one, 0, 0)
            if c < chunks - 1:
                db = db + dbi
            if c > 0:
                dc = dc + dci[c, g]
            if c == chunks - 1:
                grad[g] = carry[c, g]
            elif c > 0 or carry_ref is not None:
                grad[g] = ends[c][:, wide] * grad[g] + carry[c, g]
            db_ref[rows, thin] = db.astype(db_ref.dtype)
            dc_ref[rows, thin] = dc
    if carry_ref is not None:
        for g in range(2):
            for q in range(2):
                carry_ref[2 * g + q] = grad[g][:, q * 256 : q * 256 + 256]


def inside(length, x, dy, b, c, dt, upto, rest, kind, after, micros, name):
    n = x.shape[0]
    chunks = n // CH

    def scratch(dtype):
        return pltpu.VMEM((chunks, CH, 1024), dtype)

    has_length = length is not None
    return call(
        functools.partial(inside_kernel, chunks, has_length),
        [SMEM] * has_length + [cols(n, 1024)] * 2 + [cols(n, 128)] * 2 + [heads(n)] * 3,
        (cols(n, 1024), cols(n, 128), cols(n, 128))
        + (() if has_length else (pl.BlockSpec((4, 64, 256), lambda i: (i, 0, 0)),)),
        (
            jax.ShapeDtypeStruct(x.shape, kind),
            jax.ShapeDtypeStruct(b.shape, kind),
            jax.ShapeDtypeStruct(c.shape, F32),
        )
        + (() if has_length else (jax.ShapeDtypeStruct((16, 64, 256), F32),)),
        (*([length] if has_length else []), x, dy, b, c, dt, upto, rest),
        after,
        grid=(4,),
        scratch_shapes=[scratch(BF16)] * 4 + [scratch(F32)],
        compiler_params=limits(MOST),
        cost_estimate=cost(micros),
        name=name,
    )


def diagonal(ref, q, j):
    pair = ref[q, :, j * 128 : j * 128 + 128]
    first = halves(64)
    hi, lo = split(pair)
    zero = jnp.zeros_like(hi)
    rows = [jnp.where(first, v, zero) if h == 0 else jnp.where(first, zero, v) for v in (hi, lo) for h in (0, 1)]
    return jnp.concatenate(rows, axis=0)


def product(value, state, weight):
    res = dot(value, state, 1, 1)
    return (res[:, 0:128] + res[:, 128:256]) * weight


def start_kernel(base, dy_ref, e_ref, state_ref, part_ref, dc_ref):
    state_ref = state_ref.at[:, base : base + 64, :]
    e_turned = e_ref[0]
    pick = picker()
    out = []
    for g in range(2):
        total = None
        for q in (2 * g, 2 * g + 1):
            e = dot(e_turned, pick[:, q * 256 : q * 256 + 256], 1, 0)
            for j in range(2):
                lanes = slice(q * 256 + j * 128, q * 256 + j * 128 + 128)
                term = product(dy_ref[:, lanes], diagonal(state_ref, q, j), e[:, j * 128 : j * 128 + 128])
                total = term if total is None else total + term
        out.append(total[:, 0:64] + total[:, 64:128])
    dc_ref[...] = (part_ref[...] + jnp.concatenate(out, axis=1)).astype(BF16)


def from_start(dy, e, states, base, part, after, name):
    n = dy.shape[0]
    return call(
        functools.partial(start_kernel, base),
        [cols(n, 1024), turns(n)]
        + [pl.BlockSpec((4,) + states.shape[1:], lambda i: (i, 0, 0)), cols(n, 128)],
        (cols(n, 128),),
        (jax.ShapeDtypeStruct((n, 512), BF16),),
        (dy, e, states, part),
        after,
        grid=(4,),
        compiler_params=limits(MOST),
        cost_estimate=cost(n / 64),
        name=name,
    )


def end_kernel(base, x_ref, b_ref, w_ref, state_ref, dxp_ref, dbp_ref, dx_ref, db_ref):
    state_ref = state_ref.at[:, base : base + 64, :]
    w_turned = w_ref[0]
    pick = picker()
    out = []
    for g in range(2):
        total = None
        b_one = b_ref[:, g * 64 : g * 64 + 64]
        b_two = jnp.concatenate([b_one, b_one], axis=1)
        for q in (2 * g, 2 * g + 1):
            wide = slice(q * 256, q * 256 + 256)
            w = dot(w_turned, pick[:, wide], 1, 0)
            hi, lo = split(state_ref[q])
            dx = dot(b_two, jnp.concatenate([hi, lo], axis=0), 1, 0) * w
            dx_ref[:, wide] = (dxp_ref[:, wide] + dx).astype(BF16)
            for j in range(2):
                lanes = slice(q * 256 + j * 128, q * 256 + j * 128 + 128)
                term = product(x_ref[:, lanes], diagonal(state_ref, q, j), w[:, j * 128 : j * 128 + 128])
                total = term if total is None else total + term
        out.append(total[:, 0:64] + total[:, 64:128])
    db_ref[...] = (dbp_ref[...] + jnp.concatenate(out, axis=1)).astype(BF16)


def from_end(x, b, w, states, base, dx_part, db_part):
    n = x.shape[0]
    return call(
        functools.partial(end_kernel, base),
        [cols(n, 1024), cols(n, 128), turns(n)]
        + [pl.BlockSpec((4,) + states.shape[1:], lambda i: (i, 0, 0)), cols(n, 1024), cols(n, 128)],
        (cols(n, 1024), cols(n, 128)),
        (jax.ShapeDtypeStruct(x.shape, BF16), jax.ShapeDtypeStruct(b.shape, BF16)),
        (x, b, w, states, dx_part, db_part),
        grid=(4,),
        compiler_params=limits(MOST),
        cost_estimate=cost(10),
        name="from_end",
    )


def local(
    prompt_x,
    prompt_dt,
    head_rate,
    prompt_b,
    prompt_c,
    prompt_dy,
    branch_x,
    branch_dt,
    branch_b,
    branch_c,
    branch_dy,
    parent,
    lengths,
):
    x, dy, b, c = prompt_x[0], prompt_dy[0], prompt_b[0], prompt_c[0]
    yx, ydy, yb, yc = branch_x[0], branch_dy[0], branch_b[0], branch_c[0]
    dt, ydt = prompt_dt[0].T, branch_dt[0].T
    rate = head_rate[None, :]
    leaf = lax.axis_index("leaf")
    place = jnp.stack([leaf // 2, leaf % 2]).astype(jnp.int32)
    swap = [(s, s ^ 1) for s in range(8)]

    def turn(value):
        return lax.all_to_all(value, "seq", 0, 0, tiled=True)

    sent, upto, rest, yupto, yrest, e, w, ye = first_message(lengths, parent, rate, x, b, dt, ydy, yc, ydt)
    got = turn(sent)
    dx_part, db_part, dc_part, csent = inside(
        None, x, dy, b, c, dt, upto, rest, F32, (sent,), 28, "prompt_inside"
    )
    second, end = forward(got, csent, ())
    back = turn(second)
    keep, send = buckets(place, got, end)
    recv = lax.ppermute(send, "leaf", swap)
    m1, m2, m3, own = pack(place, end, keep, recv)
    received = [
        lax.ppermute(m, "leaf", [(s, (s + 2 * d) % 8) for s in range(8)])
        for d, m in ((1, m1), (2, m2), (3, m3))
    ]
    ydx, ydb, ydc_part = inside(
        lengths, yx, ydy, yb, yc, ydt, yupto, yrest, BF16, (own,), 14, "branch_inside"
    )
    (grads,) = states_back(
        backward_kernel, (), (got, back, own, *received), (ydb,), "end_gradients"
    )
    sent_grads = grads
    grads = turn(grads)
    (dc,) = from_start(dy, e, back, 64, dc_part, (sent_grads,), "prompt_from_start")
    (starts,) = states_back(
        starts_kernel, (place,), (got, end, recv, *received), (dc,), "branch_starts"
    )
    starts = turn(starts)
    dx, db = from_end(x, b, w, grads, 0, dx_part, db_part)
    (ydc,) = from_start(ydy, ye, starts, 0, ydc_part, (db,), "branch_from_start")
    return tuple(a[None] for a in (dx, db, dc, ydx, ydb, ydc))


def solution(mesh):
    seq = P("leaf", "seq", None)
    own = P(("seq", "leaf"), None, None)
    ids = P(("seq", "leaf"))
    in_specs = (seq, seq, P(), seq, seq, seq, own, own, own, own, own, ids, ids)
    out_specs = (seq, seq, seq, own, own, own)
    return jax.shard_map(local, mesh=mesh, in_specs=in_specs, out_specs=out_specs, check_vma=False)
```

```python
import functools
import math

import jax
import jax.numpy as jnp
from jax import lax
from jax.experimental import pallas as pl
from jax.experimental.pallas import tpu as pltpu
from jax.sharding import PartitionSpec as P

P_SIZE = 64
N = 64
CH = 128
LOG2E = math.log2(math.e)
F32 = jnp.float32
BF16 = jnp.bfloat16
BIG = 56
MOST = 62
VMEM = pl.BlockSpec(memory_space=pltpu.VMEM)
SMEM = pl.BlockSpec(memory_space=pltpu.SMEM)


def split(value):
    hi = value.astype(BF16)
    return hi, (value - hi.astype(F32)).astype(BF16)


def dot(a, b, ca, cb):
    return lax.dot_general(a, b, (((ca,), (cb,)), ((), ())), preferred_element_type=F32)


def halves(rows):
    return lax.broadcasted_iota(jnp.int32, (rows, 128), 1) < 64


def cost(micros):
    return pl.CostEstimate(flops=0, bytes_accessed=int(micros * 3.69e6), transcendentals=0)


def limits(mib):
    return pltpu.CompilerParams(vmem_limit_bytes=mib * 2**20)


def call(kernel, in_specs, out_specs, out_shape, args, after=(), **options):
    if after:
        *args, _ = lax.optimization_barrier((*args, after))
    return pl.pallas_call(
        kernel, in_specs=in_specs, out_specs=out_specs, out_shape=out_shape, **options
    )(*args)


def masked_steps(step_ref, length_ref):
    steps = step_ref[...]
    if length_ref is None:
        return steps, None
    live = lax.broadcasted_iota(jnp.int32, steps.shape, 1) < length_ref[0]
    return jnp.where(live, steps, 0.0), live


def sums(logs):
    row = lax.broadcasted_iota(jnp.int32, (CH, 2 * CH), 0)
    col = lax.broadcasted_iota(jnp.int32, (CH, 2 * CH), 1)
    ones = jnp.where((row <= col) & (col < CH) | (row > col - CH) & (col >= CH), 1.0, 0.0).astype(BF16)
    count = logs.shape[0]
    chunks = logs.shape[1] // CH
    upto, after, lasts = [], [], []
    for c in range(chunks):
        part = logs[:, c * CH : (c + 1) * CH]
        p1 = part.astype(BF16)
        rest = part - p1.astype(F32)
        p2 = rest.astype(BF16)
        p3 = (rest - p2.astype(F32)).astype(BF16)
        res = dot(jnp.concatenate([p1, p2, p3], axis=0), ones, 1, 0)
        res = res[0:count] + res[count : 2 * count] + res[2 * count : 3 * count]
        upto.append(res[:, 0:CH])
        after.append(res[:, CH:])
        lasts.append(res[:, CH - 1 : CH])
    zero = jnp.zeros((count, 1), F32)
    before, behind = [zero], [zero]
    for c in range(chunks):
        before.append(before[c] + lasts[c])
        behind.append(behind[c] + lasts[chunks - 1 - c])
    return upto, after, before[:chunks], behind[chunks - 1 :: -1] if chunks > 1 else behind[:1], before[chunks]


def picker():
    row = lax.broadcasted_iota(jnp.int32, (32, 1024), 0)
    lane = lax.broadcasted_iota(jnp.int32, (32, 1024), 1)
    return jnp.where(lane // 64 == row % 16, 1.0, 0.0).astype(BF16)


def turned(small):
    hi = small.astype(BF16).astype(F32)
    return jnp.concatenate([hi, small - hi], axis=0).T.astype(BF16)


def summary(proj_ref, weight, value_ref, out_ref, base):
    first = halves(64)
    proj_t = proj_ref[...].astype(F32).T
    for k in range(8):
        part = proj_t[(k // 4) * 64 : (k // 4) * 64 + 64]
        h0, l0 = split(part * weight[2 * k : 2 * k + 1, :])
        h1, l1 = split(part * weight[2 * k + 1 : 2 * k + 2, :])
        lhs = jnp.concatenate([h0, l0, h1, l1], axis=0)
        res = dot(lhs, value_ref[:, k * 128 : (k + 1) * 128], 1, 0)
        pair = jnp.where(first, res[0:64] + res[64:128], res[128:192] + res[192:256])
        lanes = slice((k % 2) * 128, (k % 2) * 128 + 128)
        out_ref[k // 2, base : base + 64, lanes] = pair


def first_kernel(
    len_ref,
    par_ref,
    rate_ref,
    x_ref,
    b_ref,
    dt_ref,
    ydy_ref,
    yc_ref,
    ydt_ref,
    out_ref,
    upto_ref,
    after_ref,
    yupto_ref,
    yafter_ref,
    e_ref,
    w_ref,
    ye_ref,
    w_all,
    e_all,
    ye_all,
    end_all,
):
    step = pl.program_id(0)

    @pl.when(step == 0)
    def _():
        rate = jnp.broadcast_to(rate_ref[...], (CH, 64)).T[:, 0:1] * LOG2E
        steps = dt_ref[...]
        upto, after, before, behind, end = sums(-steps * rate)
        for c in range(len(upto)):
            here = slice(c * CH, (c + 1) * CH)
            upto_ref[:, here] = upto[c]
            after_ref[:, here] = after[c]
            e_all[:, here] = jnp.exp2(upto[c] + before[c])
            w_all[:, here] = steps[:, here] * jnp.exp2(after[c] + behind[c])
        end_all[...] = jnp.exp2(jnp.broadcast_to(end, end_all.shape))
        ysteps, live = masked_steps(ydt_ref, len_ref)
        upto, after, before, _, _ = sums(-ysteps * rate)
        for c in range(len(upto)):
            here = slice(c * CH, (c + 1) * CH)
            yupto_ref[:, here] = upto[c]
            yafter_ref[:, here] = after[c]
            ye_all[:, here] = jnp.where(live[:, here], jnp.exp2(upto[c] + before[c]), 0.0)

    rows = pl.ds(pl.multiple_of(step * 16, 16), 16)
    w, ye = w_all[rows, :], ye_all[rows, :]
    summary(b_ref, w, x_ref, out_ref, 0)
    summary(yc_ref, ye, ydy_ref, out_ref, 64)
    decay = end_all[rows, :]
    parent = jnp.zeros((4, 256), F32) + par_ref[0].astype(F32)
    for q in range(4):
        out_ref[q, 128:132, :] = decay[4 * q : 4 * q + 4]
        out_ref[q, 132:136, :] = parent
    e_ref[0] = turned(e_all[rows, :])
    w_ref[0] = turned(w)
    ye_ref[0] = turned(ye)


def cols(n, w):
    return pl.BlockSpec((n, w), lambda i: (0, i))


def heads(n):
    return pl.BlockSpec((16, n), lambda i: (i, 0))


def whole(*shape):
    return pl.BlockSpec(shape, lambda i: (0,) * len(shape))


def turns(n):
    return pl.BlockSpec((1, n, 32), lambda i: (i, 0, 0))


def first_message(length, parent, rate, x, b, dt, ydy, yc, ydt):
    n, m = x.shape[0], ydy.shape[0]
    f32 = lambda *shape: jax.ShapeDtypeStruct(shape, F32)
    bf16 = lambda *shape: jax.ShapeDtypeStruct(shape, BF16)
    return call(
        first_kernel,
        [SMEM, SMEM, whole(1, 64), cols(n, 1024), cols(n, 128), whole(64, n)]
        + [cols(m, 1024), cols(m, 128), whole(64, m)],
        (pl.BlockSpec((4, 136, 256), lambda i: (i, 0, 0)),)
        + (whole(64, n),) * 2
        + (whole(64, m),) * 2
        + (turns(n), turns(n), turns(m)),
        (f32(16, 136, 256), f32(64, n), f32(64, n), f32(64, m), f32(64, m))
        + (bf16(4, n, 32), bf16(4, n, 32), bf16(4, m, 32)),
        (length, parent, rate, x, b, dt, ydy, yc, ydt),
        grid=(4,),
        scratch_shapes=[
            pltpu.VMEM((64, n), F32),
            pltpu.VMEM((64, n), F32),
            pltpu.VMEM((64, m), F32),
            pltpu.VMEM((64, 256), F32),
        ],
        compiler_params=limits(BIG),
        cost_estimate=cost(8),
        name="first_message",
    )


def decay_row(got_ref, i, at):
    lane = lax.broadcasted_iota(jnp.int32, (1, 256), 1)
    row = [got_ref[i, at + q : at + q + 1, :] for q in range(4)]
    low = jnp.where(lane < 64, row[0], row[1])
    return jnp.where(lane < 128, low, jnp.where(lane < 192, row[2], row[3]))


def forward_kernel(got_ref, carry_ref, out_ref, end_ref):
    state = jnp.zeros((64, 256), F32)
    for i in range(16):
        out_ref[i, 0:64, :] = carry_ref[i]
        out_ref[i, 64:128, :] = state
        state = decay_row(got_ref, i, 128) * state + got_ref[i, 0:64, :]
    end_ref[...] = state


def forward(got, carry, after):
    return call(
        forward_kernel,
        [VMEM] * 2,
        (VMEM,) * 2,
        (jax.ShapeDtypeStruct((16, 128, 256), F32), jax.ShapeDtypeStruct((64, 256), F32)),
        (got, carry),
        after,
        compiler_params=limits(12),
        cost_estimate=cost(1),
        name="forward_scan",
    )


def buckets_kernel(place_ref, got_ref, end_ref, keep_ref, send_ref):
    core = place_ref[1].astype(F32)
    send_ref[4] = end_ref[...]
    for z in range(4):
        keep = jnp.zeros((64, 256), F32)
        send = jnp.zeros((64, 256), F32)
        for i in range(16):
            owner = got_ref[i, 132:133, :] - 2.0 * z
            term = got_ref[i, 64:128, :]
            keep = keep + jnp.where(owner == core, term, 0.0)
            send = send + jnp.where(owner == 1.0 - core, term, 0.0)
        keep_ref[z] = keep
        send_ref[z] = send


def buckets(place, got, end):
    return call(
        buckets_kernel,
        [SMEM, VMEM, VMEM],
        (VMEM,) * 2,
        (jax.ShapeDtypeStruct((4, 64, 256), F32), jax.ShapeDtypeStruct((5, 64, 256), F32)),
        (place, got, end),
        compiler_params=limits(12),
        cost_estimate=cost(1),
        name="buckets",
    )


def pack_kernel(place_ref, end_ref, keep_ref, recv_ref, m1_ref, m2_ref, m3_ref, own_ref):
    z = place_ref[0]
    own_ref[...] = keep_ref[z] + recv_ref[z]
    for d, ref in ((1, m1_ref), (2, m2_ref), (3, m3_ref)):
        to = lax.rem(z + d, 4)
        ref[0] = end_ref[...]
        ref[1] = recv_ref[4]
        ref[2] = keep_ref[to] + recv_ref[to]


def pack(place, end, keep, recv):
    msg = jax.ShapeDtypeStruct((3, 64, 256), F32)
    return call(
        pack_kernel,
        [SMEM] + [VMEM] * 3,
        (VMEM,) * 4,
        (msg, msg, msg, jax.ShapeDtypeStruct((64, 256), F32)),
        (place, end, keep, recv),
        compiler_params=limits(12),
        cost_estimate=cost(1),
        name="pack_leaf",
    )


def backward_kernel(
    place_ref, rows_ref, carry_ref, end_ref, recv_ref, own_ref, r1, r2, r3, out_ref
):
    z = place_ref[0]
    core = place_ref[1]
    grad = own_ref[...] + r1[2] + r2[2] + r3[2]
    for i in range(15, -1, -1):
        out_ref[i, 0:64, :] = grad
        grad = decay_row(rows_ref, i, 0) * grad + carry_ref[i]
    mine = (end_ref[...], r1[0], r2[0], r3[0])
    theirs = (recv_ref[4], r1[1], r2[1], r3[1])
    for i in range(16):
        owner = rows_ref[i, 4:5, :]
        start = jnp.zeros((64, 256), F32)
        for d in range(4):
            place = 2 * lax.rem(z + 4 - d, 4)
            here = (place + core).astype(F32)
            there = (place + 1 - core).astype(F32)
            start = start + jnp.where(owner == here, mine[d], 0.0)
            start = start + jnp.where(owner == there, theirs[d], 0.0)
        out_ref[i, 64:128, :] = start


def backward(place, got, carry, end, recv, own, received):
    return call(
        backward_kernel,
        [
            SMEM,
            pl.BlockSpec((16, 8, 256), lambda i: (0, 16, 0)),
            pl.BlockSpec((16, 64, 256), lambda i: (0, 0, 0)),
            whole(64, 256),
            whole(5, 64, 256),
            whole(64, 256),
        ]
        + [whole(3, 64, 256)] * 3,
        (whole(16, 128, 256),),
        (jax.ShapeDtypeStruct((16, 128, 256), F32),),
        (place, got, carry, end, recv, own, *received),
        grid=(1,),
        compiler_params=limits(16),
        cost_estimate=cost(2),
        name="backward_scan",
    )


def inside_kernel(chunks, has_length, *refs):
    if has_length:
        len_ref, refs = refs[0], refs[1:]
    else:
        len_ref = None
    x_ref, dy_ref, b_ref, c_ref, dt_ref, upto_ref, after_ref, dx_ref, db_ref, dc_ref = refs[:10]
    if has_length:
        carry_ref = None
        xh, xl, yh, yl, weight = refs[10:]
    else:
        carry_ref = refs[10]
        xh, xl, yh, yl, weight = refs[11:]
    pick = picker()
    first = halves(CH)
    causal = lax.broadcasted_iota(jnp.int32, (CH, CH), 1) >= lax.broadcasted_iota(
        jnp.int32, (CH, CH), 0
    )
    steps, _ = masked_steps(dt_ref, len_ref)
    upto = [upto_ref[:, c * CH : (c + 1) * CH] for c in range(chunks)]
    after = [after_ref[:, c * CH : (c + 1) * CH] for c in range(chunks)]
    state = [jnp.zeros((64, 512), F32)] * 2
    carry, ends, dci = {}, {}, {}

    def grads_out(c):
        dy = dy_ref[c * CH : (c + 1) * CH, :]
        if len_ref is None:
            return dy
        token = lax.broadcasted_iota(jnp.int32, (CH, 1024), 0) + c * CH
        return jnp.where(token < len_ref[0], dy.astype(F32), 0.0).astype(BF16)

    def cross(lhs_hi, lhs_lo, rhs):
        hi, lo = split(rhs)
        res = dot(lhs_hi, jnp.concatenate([hi, lo], axis=0), 1, 1)
        return res[:, 0:64] + res[:, 64:128] + dot(lhs_lo, hi, 1, 1)

    for c in range(chunks):
        rows = slice(c * CH, (c + 1) * CH)
        rate_c = steps[:, rows]
        w_turned = turned(rate_c * jnp.exp2(after[c]))
        e_turned = turned(jnp.exp2(upto[c]))
        dy_c = grads_out(c)
        tails = []
        for q in range(4):
            lanes = slice(q * 256, q * 256 + 256)
            w = dot(w_turned, pick[:, lanes], 1, 0)
            weight[c, :, lanes] = w
            xh[c, :, lanes], xl[c, :, lanes] = split(w * x_ref[rows, lanes].astype(F32))
            e = dot(e_turned, pick[:, lanes], 1, 0)
            tails.append(e[CH - 1 : CH])
            yh[c, :, lanes], yl[c, :, lanes] = split(e * dy_c[:, lanes].astype(F32))
        ends[c] = jnp.concatenate(tails, axis=1)
        for g in range(2):
            wide = slice(g * 512, g * 512 + 512)
            thin = slice(g * 64, g * 64 + 64)
            if c > 0:
                dci[c, g] = cross(yh[c, :, wide], yl[c, :, wide], state[g])
            if c < chunks - 1:
                b_one = b_ref[rows, thin]
                added = dot(b_one, xh[c, :, wide], 0, 0) + dot(b_one, xl[c, :, wide], 0, 0)
                state[g] = added if c == 0 else ends[c][:, wide] * state[g] + added
            if c > 0 or carry_ref is not None:
                c_one = c_ref[rows, thin]
                carry[c, g] = dot(c_one, yh[c, :, wide], 0, 0) + dot(c_one, yl[c, :, wide], 0, 0)
    grad = [None, None]
    for c in range(chunks - 1, -1, -1):
        rows = slice(c * CH, (c + 1) * CH)
        cum_t = upto[c]
        cum_s = cum_t.T
        rate_s = steps[:, rows].T
        dy_c = grads_out(c)
        for g in range(2):
            wide = slice(g * 512, g * 512 + 512)
            thin = slice(g * 64, g * 64 + 64)
            b_one = b_ref[rows, thin]
            c_one = c_ref[rows, thin]
            dxi = None
            if c < chunks - 1:
                hi, lo = split(grad[g])
                dxi = dot(
                    jnp.concatenate([b_one, b_one], axis=1),
                    jnp.concatenate([hi, lo], axis=0),
                    1,
                    0,
                )
                dxi = dxi * weight[c, :, wide]
                dbi = cross(xh[c, :, wide], xl[c, :, wide], grad[g])
            scores = dot(b_one, c_one, 1, 1)
            total = jnp.zeros((CH, CH), F32)
            for k in range(4):
                lanes = slice(g * 512 + k * 128, g * 512 + k * 128 + 128)
                dy = dy_c[:, lanes]
                zero = jnp.zeros_like(dy)
                stacked = jnp.concatenate(
                    [jnp.where(first, dy, zero), jnp.where(first, zero, dy)], axis=0
                )
                pairs = dot(x_ref[rows, lanes], stacked, 1, 1)
                his, los = [], []
                for e in range(2):
                    h = g * 8 + 2 * k + e
                    gap = cum_t[h : h + 1, :] - jnp.broadcast_to(cum_s[:, h : h + 1], (CH, CH))
                    decay = jnp.exp2(jnp.where(causal, gap, -jnp.inf))
                    decay = decay * jnp.broadcast_to(rate_s[:, h : h + 1], (CH, CH))
                    total = total + decay * pairs[:, e * CH : (e + 1) * CH]
                    hi, lo = split(decay * scores)
                    his.append(hi)
                    los.append(lo)
                lhs = jnp.concatenate(
                    [jnp.concatenate(his, axis=1), jnp.concatenate(los, axis=1)], axis=0
                )
                res = dot(lhs, stacked, 1, 0)
                dx = res[0:CH] + res[CH : 2 * CH]
                if dxi is not None:
                    dx = dx + dxi[:, k * 128 : k * 128 + 128]
                dx_ref[rows, lanes] = dx.astype(dx_ref.dtype)
            hi, lo = split(total)
            db = dot(hi, c_one, 1, 0) + dot(lo, c_one, 1, 0)
            dc = dot(hi, b_one, 0, 0) + dot(lo, b_one, 0, 0)
            if c < chunks - 1:
                db = db + dbi
            if c > 0:
                dc = dc + dci[c, g]
            if c == chunks - 1:
                grad[g] = carry[c, g]
            elif c > 0 or carry_ref is not None:
                grad[g] = ends[c][:, wide] * grad[g] + carry[c, g]
            db_ref[rows, thin] = db.astype(db_ref.dtype)
            dc_ref[rows, thin] = dc
    if carry_ref is not None:
        for g in range(2):
            for q in range(2):
                carry_ref[2 * g + q] = grad[g][:, q * 256 : q * 256 + 256]


def inside(length, x, dy, b, c, dt, upto, rest, kind, after, micros, name):
    n = x.shape[0]
    chunks = n // CH

    def scratch(dtype):
        return pltpu.VMEM((chunks, CH, 1024), dtype)

    has_length = length is not None
    return call(
        functools.partial(inside_kernel, chunks, has_length),
        [SMEM] * has_length + [cols(n, 1024)] * 2 + [cols(n, 128)] * 2 + [heads(n)] * 3,
        (cols(n, 1024), cols(n, 128), cols(n, 128))
        + (() if has_length else (pl.BlockSpec((4, 64, 256), lambda i: (i, 0, 0)),)),
        (
            jax.ShapeDtypeStruct(x.shape, kind),
            jax.ShapeDtypeStruct(b.shape, kind),
            jax.ShapeDtypeStruct(c.shape, F32),
        )
        + (() if has_length else (jax.ShapeDtypeStruct((16, 64, 256), F32),)),
        (*([length] if has_length else []), x, dy, b, c, dt, upto, rest),
        after,
        grid=(4,),
        scratch_shapes=[scratch(BF16)] * 4 + [scratch(F32)],
        compiler_params=limits(MOST if has_length else BIG),
        cost_estimate=cost(micros),
        name=name,
    )


def diagonal(ref, q, j):
    pair = ref[q, :, j * 128 : j * 128 + 128]
    first = halves(64)
    hi, lo = split(pair)
    zero = jnp.zeros_like(hi)
    rows = [jnp.where(first, v, zero) if h == 0 else jnp.where(first, zero, v) for v in (hi, lo) for h in (0, 1)]
    return jnp.concatenate(rows, axis=0)


def product(value, state, weight):
    res = dot(value, state, 1, 1)
    return (res[:, 0:128] + res[:, 128:256]) * weight


def start_kernel(base, dy_ref, e_ref, state_ref, part_ref, dc_ref):
    state_ref = state_ref.at[:, base : base + 64, :]
    e_turned = e_ref[0]
    pick = picker()
    out = []
    for g in range(2):
        total = None
        for q in (2 * g, 2 * g + 1):
            e = dot(e_turned, pick[:, q * 256 : q * 256 + 256], 1, 0)
            for j in range(2):
                lanes = slice(q * 256 + j * 128, q * 256 + j * 128 + 128)
                term = product(dy_ref[:, lanes], diagonal(state_ref, q, j), e[:, j * 128 : j * 128 + 128])
                total = term if total is None else total + term
        out.append(total[:, 0:64] + total[:, 64:128])
    dc_ref[...] = (part_ref[...] + jnp.concatenate(out, axis=1)).astype(BF16)


def from_start(dy, e, states, base, part, after, name):
    n = dy.shape[0]
    return call(
        functools.partial(start_kernel, base),
        [cols(n, 1024), turns(n)]
        + [pl.BlockSpec((4,) + states.shape[1:], lambda i: (i, 0, 0)), cols(n, 128)],
        (cols(n, 128),),
        (jax.ShapeDtypeStruct((n, 512), BF16),),
        (dy, e, states, part),
        after,
        grid=(4,),
        compiler_params=limits(MOST),
        cost_estimate=cost(n / 64),
        name=name,
    )


def end_kernel(base, x_ref, b_ref, w_ref, state_ref, dxp_ref, dbp_ref, dx_ref, db_ref):
    state_ref = state_ref.at[:, base : base + 64, :]
    w_turned = w_ref[0]
    pick = picker()
    out = []
    for g in range(2):
        total = None
        b_one = b_ref[:, g * 64 : g * 64 + 64]
        b_two = jnp.concatenate([b_one, b_one], axis=1)
        for q in (2 * g, 2 * g + 1):
            wide = slice(q * 256, q * 256 + 256)
            w = dot(w_turned, pick[:, wide], 1, 0)
            hi, lo = split(state_ref[q])
            dx = dot(b_two, jnp.concatenate([hi, lo], axis=0), 1, 0) * w
            dx_ref[:, wide] = (dxp_ref[:, wide] + dx).astype(BF16)
            for j in range(2):
                lanes = slice(q * 256 + j * 128, q * 256 + j * 128 + 128)
                term = product(x_ref[:, lanes], diagonal(state_ref, q, j), w[:, j * 128 : j * 128 + 128])
                total = term if total is None else total + term
        out.append(total[:, 0:64] + total[:, 64:128])
    db_ref[...] = (dbp_ref[...] + jnp.concatenate(out, axis=1)).astype(BF16)


def tail_kernel(
    x_ref, b_ref, w_ref, state_ref, dxp_ref, dbp_ref, ydy_ref, ye_ref, ydcp_ref, dx_ref, db_ref, ydc_ref
):
    end_kernel(0, x_ref, b_ref, w_ref, state_ref, dxp_ref, dbp_ref, dx_ref, db_ref)
    start_kernel(64, ydy_ref, ye_ref, state_ref, ydcp_ref, ydc_ref)


def from_states(x, b, w, states, dx_part, db_part, ydy, ye, ydc_part):
    n, m = x.shape[0], ydy.shape[0]
    return call(
        tail_kernel,
        [cols(n, 1024), cols(n, 128), turns(n)]
        + [pl.BlockSpec((4, 128, 256), lambda i: (i, 0, 0)), cols(n, 1024), cols(n, 128)]
        + [cols(m, 1024), turns(m), cols(m, 128)],
        (cols(n, 1024), cols(n, 128), cols(m, 128)),
        (
            jax.ShapeDtypeStruct(x.shape, BF16),
            jax.ShapeDtypeStruct(b.shape, BF16),
            jax.ShapeDtypeStruct((m, 512), BF16),
        ),
        (x, b, w, states, dx_part, db_part, ydy, ye, ydc_part),
        grid=(4,),
        compiler_params=limits(MOST),
        cost_estimate=cost(12),
        name="from_states",
    )


def local(
    prompt_x,
    prompt_dt,
    head_rate,
    prompt_b,
    prompt_c,
    prompt_dy,
    branch_x,
    branch_dt,
    branch_b,
    branch_c,
    branch_dy,
    parent,
    lengths,
):
    x, dy, b, c = prompt_x[0], prompt_dy[0], prompt_b[0], prompt_c[0]
    yx, ydy, yb, yc = branch_x[0], branch_dy[0], branch_b[0], branch_c[0]
    dt, ydt = prompt_dt[0].T, branch_dt[0].T
    rate = head_rate[None, :]
    leaf = lax.axis_index("leaf")
    place = jnp.stack([leaf // 2, leaf % 2]).astype(jnp.int32)
    swap = [(s, s ^ 1) for s in range(8)]

    def turn(value):
        return lax.all_to_all(value, "seq", 0, 0, tiled=True)

    sent, upto, rest, yupto, yrest, e, w, ye = first_message(lengths, parent, rate, x, b, dt, ydy, yc, ydt)
    got = turn(sent)
    dx_part, db_part, dc_part, csent = inside(
        None, x, dy, b, c, dt, upto, rest, F32, (sent,), 28, "prompt_inside"
    )
    second, end = forward(got, csent, ())
    back = turn(second)
    keep, send = buckets(place, got, end)
    recv = lax.ppermute(send, "leaf", swap)
    m1, m2, m3, own = pack(place, end, keep, recv)
    received = [
        lax.ppermute(m, "leaf", [(s, (s + 2 * d) % 8) for s in range(8)])
        for d, m in ((1, m1), (2, m2), (3, m3))
    ]
    (third,) = backward(place, got, back, end, recv, own, received)
    states = turn(third)
    (dc,) = from_start(dy, e, back, 64, dc_part, (third,), "prompt_from_start")
    ydx, ydb, ydc_part = inside(
        lengths, yx, ydy, yb, yc, ydt, yupto, yrest, BF16, (dc,), 14, "branch_inside"
    )
    dx, db, ydc = from_states(x, b, w, states, dx_part, db_part, ydy, ye, ydc_part)
    return tuple(a[None] for a in (dx, db, dc, ydx, ydb, ydc))


def solution(mesh):
    seq = P("leaf", "seq", None)
    own = P(("seq", "leaf"), None, None)
    ids = P(("seq", "leaf"))
    in_specs = (seq, seq, P(), seq, seq, seq, own, own, own, own, own, ids, ids)
    out_specs = (seq, seq, seq, own, own, own)
    return jax.shard_map(local, mesh=mesh, in_specs=in_specs, out_specs=out_specs, check_vma=False)
```

```python
import functools
import math

import jax
import jax.numpy as jnp
from jax import lax
from jax.experimental import pallas as pl
from jax.experimental.pallas import tpu as pltpu
from jax.sharding import PartitionSpec as P

P_SIZE = 64
N = 64
CH = 128
LOG2E = math.log2(math.e)
F32 = jnp.float32
BF16 = jnp.bfloat16
BIG = 56
MOST = 62
VMEM = pl.BlockSpec(memory_space=pltpu.VMEM)
SMEM = pl.BlockSpec(memory_space=pltpu.SMEM)


def split(value):
    hi = value.astype(BF16)
    return hi, (value - hi.astype(F32)).astype(BF16)


def dot(a, b, ca, cb):
    return lax.dot_general(a, b, (((ca,), (cb,)), ((), ())), preferred_element_type=F32)


def halves(rows):
    return lax.broadcasted_iota(jnp.int32, (rows, 128), 1) < 64


def cost(micros):
    return pl.CostEstimate(flops=0, bytes_accessed=int(micros * 3.69e6), transcendentals=0)


def limits(mib):
    return pltpu.CompilerParams(vmem_limit_bytes=mib * 2**20)


def call(kernel, in_specs, out_specs, out_shape, args, after=(), **options):
    if after:
        *args, _ = lax.optimization_barrier((*args, after))
    return pl.pallas_call(
        kernel, in_specs=in_specs, out_specs=out_specs, out_shape=out_shape, **options
    )(*args)


def masked_steps(step_ref, length_ref):
    steps = step_ref[...]
    if length_ref is None:
        return steps, None
    live = lax.broadcasted_iota(jnp.int32, steps.shape, 1) < length_ref[0]
    return jnp.where(live, steps, 0.0), live


def sums(logs):
    row = lax.broadcasted_iota(jnp.int32, (CH, 2 * CH), 0)
    col = lax.broadcasted_iota(jnp.int32, (CH, 2 * CH), 1)
    ones = jnp.where((row <= col) & (col < CH) | (row > col - CH) & (col >= CH), 1.0, 0.0).astype(BF16)
    count = logs.shape[0]
    chunks = logs.shape[1] // CH
    upto, after, lasts = [], [], []
    for c in range(chunks):
        part = logs[:, c * CH : (c + 1) * CH]
        p1 = part.astype(BF16)
        rest = part - p1.astype(F32)
        p2 = rest.astype(BF16)
        p3 = (rest - p2.astype(F32)).astype(BF16)
        res = dot(jnp.concatenate([p1, p2, p3], axis=0), ones, 1, 0)
        res = res[0:count] + res[count : 2 * count] + res[2 * count : 3 * count]
        upto.append(res[:, 0:CH])
        after.append(res[:, CH:])
        lasts.append(res[:, CH - 1 : CH])
    zero = jnp.zeros((count, 1), F32)
    before, behind = [zero], [zero]
    for c in range(chunks):
        before.append(before[c] + lasts[c])
        behind.append(behind[c] + lasts[chunks - 1 - c])
    return upto, after, before[:chunks], behind[chunks - 1 :: -1] if chunks > 1 else behind[:1], before[chunks]


def picker():
    row = lax.broadcasted_iota(jnp.int32, (32, 1024), 0)
    lane = lax.broadcasted_iota(jnp.int32, (32, 1024), 1)
    return jnp.where(lane // 64 == row % 16, 1.0, 0.0).astype(BF16)


def turned(small):
    hi = small.astype(BF16).astype(F32)
    return jnp.concatenate([hi, small - hi], axis=0).T.astype(BF16)


def summary(proj_ref, weight, value_ref, out_ref, base):
    first = halves(64)
    proj_t = proj_ref[...].astype(F32).T
    for k in range(8):
        part = proj_t[(k // 4) * 64 : (k // 4) * 64 + 64]
        h0, l0 = split(part * weight[2 * k : 2 * k + 1, :])
        h1, l1 = split(part * weight[2 * k + 1 : 2 * k + 2, :])
        lhs = jnp.concatenate([h0, l0, h1, l1], axis=0)
        res = dot(lhs, value_ref[:, k * 128 : (k + 1) * 128], 1, 0)
        pair = jnp.where(first, res[0:64] + res[64:128], res[128:192] + res[192:256])
        lanes = slice((k % 2) * 128, (k % 2) * 128 + 128)
        out_ref[k // 2, base : base + 64, lanes] = pair


def first_kernel(
    len_ref,
    par_ref,
    rate_ref,
    x_ref,
    b_ref,
    dt_ref,
    ydy_ref,
    yc_ref,
    ydt_ref,
    out_ref,
    upto_ref,
    after_ref,
    yupto_ref,
    yafter_ref,
    e_ref,
    w_ref,
    ye_ref,
    w_all,
    e_all,
    ye_all,
    end_all,
):
    step = pl.program_id(0)

    @pl.when(step == 0)
    def _():
        rate = jnp.broadcast_to(rate_ref[...], (CH, 64)).T[:, 0:1] * LOG2E
        steps = dt_ref[...]
        upto, after, before, behind, end = sums(-steps * rate)
        for c in range(len(upto)):
            here = slice(c * CH, (c + 1) * CH)
            upto_ref[:, here] = upto[c]
            after_ref[:, here] = after[c]
            e_all[:, here] = jnp.exp2(upto[c] + before[c])
            w_all[:, here] = steps[:, here] * jnp.exp2(after[c] + behind[c])
        end_all[...] = jnp.exp2(jnp.broadcast_to(end, end_all.shape))
        ysteps, live = masked_steps(ydt_ref, len_ref)
        upto, after, before, _, _ = sums(-ysteps * rate)
        for c in range(len(upto)):
            here = slice(c * CH, (c + 1) * CH)
            yupto_ref[:, here] = upto[c]
            yafter_ref[:, here] = after[c]
            ye_all[:, here] = jnp.where(live[:, here], jnp.exp2(upto[c] + before[c]), 0.0)

    rows = pl.ds(pl.multiple_of(step * 16, 16), 16)
    w, ye = w_all[rows, :], ye_all[rows, :]
    summary(b_ref, w, x_ref, out_ref, 0)
    summary(yc_ref, ye, ydy_ref, out_ref, 64)
    decay = end_all[rows, :]
    parent = jnp.zeros((4, 256), F32) + par_ref[0].astype(F32)
    for q in range(4):
        out_ref[q, 128:132, :] = decay[4 * q : 4 * q + 4]
        out_ref[q, 132:136, :] = parent
    e_ref[0] = turned(e_all[rows, :])
    w_ref[0] = turned(w)
    ye_ref[0] = turned(ye)


def cols(n, w):
    return pl.BlockSpec((n, w), lambda i: (0, i))


def heads(n):
    return pl.BlockSpec((16, n), lambda i: (i, 0))


def whole(*shape):
    return pl.BlockSpec(shape, lambda i: (0,) * len(shape))


def turns(n):
    return pl.BlockSpec((1, n, 32), lambda i: (i, 0, 0))


def first_message(length, parent, rate, x, b, dt, ydy, yc, ydt):
    n, m = x.shape[0], ydy.shape[0]
    f32 = lambda *shape: jax.ShapeDtypeStruct(shape, F32)
    bf16 = lambda *shape: jax.ShapeDtypeStruct(shape, BF16)
    return call(
        first_kernel,
        [SMEM, SMEM, whole(1, 64), cols(n, 1024), cols(n, 128), whole(64, n)]
        + [cols(m, 1024), cols(m, 128), whole(64, m)],
        (pl.BlockSpec((4, 136, 256), lambda i: (i, 0, 0)),)
        + (whole(64, n),) * 2
        + (whole(64, m),) * 2
        + (turns(n), turns(n), turns(m)),
        (f32(16, 136, 256), f32(64, n), f32(64, n), f32(64, m), f32(64, m))
        + (bf16(4, n, 32), bf16(4, n, 32), bf16(4, m, 32)),
        (length, parent, rate, x, b, dt, ydy, yc, ydt),
        grid=(4,),
        scratch_shapes=[
            pltpu.VMEM((64, n), F32),
            pltpu.VMEM((64, n), F32),
            pltpu.VMEM((64, m), F32),
            pltpu.VMEM((64, 256), F32),
        ],
        compiler_params=limits(BIG),
        cost_estimate=cost(8),
        name="first_message",
    )


def decay_row(got_ref, i, at):
    lane = lax.broadcasted_iota(jnp.int32, (1, 256), 1)
    row = [got_ref[i, at + q : at + q + 1, :] for q in range(4)]
    low = jnp.where(lane < 64, row[0], row[1])
    return jnp.where(lane < 128, low, jnp.where(lane < 192, row[2], row[3]))


def forward_kernel(got_ref, carry_ref, out_ref, end_ref):
    state = jnp.zeros((64, 256), F32)
    for i in range(16):
        out_ref[i, 0:64, :] = carry_ref[i]
        out_ref[i, 64:128, :] = state
        state = decay_row(got_ref, i, 128) * state + got_ref[i, 0:64, :]
    end_ref[...] = state


def forward(got, carry, after):
    return call(
        forward_kernel,
        [VMEM] * 2,
        (VMEM,) * 2,
        (jax.ShapeDtypeStruct((16, 128, 256), F32), jax.ShapeDtypeStruct((64, 256), F32)),
        (got, carry),
        after,
        compiler_params=limits(12),
        cost_estimate=cost(1),
        name="forward_scan",
    )


def buckets_kernel(place_ref, got_ref, end_ref, keep_ref, send_ref):
    core = place_ref[1].astype(F32)
    send_ref[4] = end_ref[...]
    for z in range(4):
        keep = jnp.zeros((64, 256), F32)
        send = jnp.zeros((64, 256), F32)
        for i in range(16):
            owner = got_ref[i, 132:133, :] - 2.0 * z
            term = got_ref[i, 64:128, :]
            keep = keep + jnp.where(owner == core, term, 0.0)
            send = send + jnp.where(owner == 1.0 - core, term, 0.0)
        keep_ref[z] = keep
        send_ref[z] = send


def buckets(place, got, end):
    return call(
        buckets_kernel,
        [SMEM, VMEM, VMEM],
        (VMEM,) * 2,
        (jax.ShapeDtypeStruct((4, 64, 256), F32), jax.ShapeDtypeStruct((5, 64, 256), F32)),
        (place, got, end),
        compiler_params=limits(12),
        cost_estimate=cost(1),
        name="buckets",
    )


def pack_kernel(place_ref, end_ref, keep_ref, recv_ref, m1_ref, m2_ref, m3_ref, own_ref):
    z = place_ref[0]
    own_ref[...] = keep_ref[z] + recv_ref[z]
    for d, ref in ((1, m1_ref), (2, m2_ref), (3, m3_ref)):
        to = lax.rem(z + d, 4)
        ref[0] = end_ref[...]
        ref[1] = recv_ref[4]
        ref[2] = keep_ref[to] + recv_ref[to]


def pack(place, end, keep, recv):
    msg = jax.ShapeDtypeStruct((3, 64, 256), F32)
    return call(
        pack_kernel,
        [SMEM] + [VMEM] * 3,
        (VMEM,) * 4,
        (msg, msg, msg, jax.ShapeDtypeStruct((64, 256), F32)),
        (place, end, keep, recv),
        compiler_params=limits(12),
        cost_estimate=cost(1),
        name="pack_leaf",
    )


def backward_kernel(
    place_ref, rows_ref, carry_ref, end_ref, recv_ref, own_ref, r1, r2, r3, out_ref
):
    z = place_ref[0]
    core = place_ref[1]
    grad = own_ref[...] + r1[2] + r2[2] + r3[2]
    for i in range(15, -1, -1):
        out_ref[i, 0:64, :] = grad
        grad = decay_row(rows_ref, i, 0) * grad + carry_ref[i]
    mine = (end_ref[...], r1[0], r2[0], r3[0])
    theirs = (recv_ref[4], r1[1], r2[1], r3[1])
    for i in range(16):
        owner = rows_ref[i, 4:5, :]
        start = jnp.zeros((64, 256), F32)
        for d in range(4):
            place = 2 * lax.rem(z + 4 - d, 4)
            here = (place + core).astype(F32)
            there = (place + 1 - core).astype(F32)
            start = start + jnp.where(owner == here, mine[d], 0.0)
            start = start + jnp.where(owner == there, theirs[d], 0.0)
        out_ref[i, 64:128, :] = start


def backward(place, got, carry, end, recv, own, received):
    return call(
        backward_kernel,
        [
            SMEM,
            pl.BlockSpec((16, 8, 256), lambda i: (0, 16, 0)),
            pl.BlockSpec((16, 64, 256), lambda i: (0, 0, 0)),
            whole(64, 256),
            whole(5, 64, 256),
            whole(64, 256),
        ]
        + [whole(3, 64, 256)] * 3,
        (whole(16, 128, 256),),
        (jax.ShapeDtypeStruct((16, 128, 256), F32),),
        (place, got, carry, end, recv, own, *received),
        grid=(1,),
        compiler_params=limits(16),
        cost_estimate=cost(2),
        name="backward_scan",
    )


def inside_kernel(chunks, has_length, *refs):
    if has_length:
        len_ref, refs = refs[0], refs[1:]
    else:
        len_ref = None
    x_ref, dy_ref, b_ref, c_ref, dt_ref, upto_ref, after_ref, dx_ref, db_ref, dc_ref = refs[:10]
    if has_length:
        carry_ref = None
        xh, xl, yh, yl, weight = refs[10:]
    else:
        carry_ref = refs[10]
        xh, xl, yh, yl, weight = refs[11:]
    pick = picker()
    first = halves(CH)
    causal = lax.broadcasted_iota(jnp.int32, (CH, CH), 1) >= lax.broadcasted_iota(
        jnp.int32, (CH, CH), 0
    )
    steps, _ = masked_steps(dt_ref, len_ref)
    upto = [upto_ref[:, c * CH : (c + 1) * CH] for c in range(chunks)]
    after = [after_ref[:, c * CH : (c + 1) * CH] for c in range(chunks)]
    state = [jnp.zeros((64, 512), F32)] * 2
    carry, ends, dci = {}, {}, {}

    def grads_out(c):
        dy = dy_ref[c * CH : (c + 1) * CH, :]
        if len_ref is None:
            return dy
        token = lax.broadcasted_iota(jnp.int32, (CH, 1024), 0) + c * CH
        return jnp.where(token < len_ref[0], dy.astype(F32), 0.0).astype(BF16)

    def cross(lhs_hi, lhs_lo, rhs):
        hi, lo = split(rhs)
        res = dot(lhs_hi, jnp.concatenate([hi, lo], axis=0), 1, 1)
        return res[:, 0:64] + res[:, 64:128] + dot(lhs_lo, hi, 1, 1)

    for c in range(chunks):
        rows = slice(c * CH, (c + 1) * CH)
        rate_c = steps[:, rows]
        w_turned = turned(rate_c * jnp.exp2(after[c]))
        e_turned = turned(jnp.exp2(upto[c]))
        dy_c = grads_out(c)
        tails = []
        for q in range(4):
            lanes = slice(q * 256, q * 256 + 256)
            w = dot(w_turned, pick[:, lanes], 1, 0)
            weight[c, :, lanes] = w
            xh[c, :, lanes], xl[c, :, lanes] = split(w * x_ref[rows, lanes].astype(F32))
            e = dot(e_turned, pick[:, lanes], 1, 0)
            tails.append(e[CH - 1 : CH])
            yh[c, :, lanes], yl[c, :, lanes] = split(e * dy_c[:, lanes].astype(F32))
        ends[c] = jnp.concatenate(tails, axis=1)
        for g in range(2):
            wide = slice(g * 512, g * 512 + 512)
            thin = slice(g * 64, g * 64 + 64)
            if c > 0:
                dci[c, g] = cross(yh[c, :, wide], yl[c, :, wide], state[g])
            if c < chunks - 1:
                b_one = b_ref[rows, thin]
                added = dot(b_one, xh[c, :, wide], 0, 0) + dot(b_one, xl[c, :, wide], 0, 0)
                state[g] = added if c == 0 else ends[c][:, wide] * state[g] + added
            if c > 0 or carry_ref is not None:
                c_one = c_ref[rows, thin]
                carry[c, g] = dot(c_one, yh[c, :, wide], 0, 0) + dot(c_one, yl[c, :, wide], 0, 0)
    grad = [None, None]
    for c in range(chunks - 1, -1, -1):
        rows = slice(c * CH, (c + 1) * CH)
        cum_t = upto[c]
        cum_s = cum_t.T
        rate_s = steps[:, rows].T
        dy_c = grads_out(c)
        for g in range(2):
            wide = slice(g * 512, g * 512 + 512)
            thin = slice(g * 64, g * 64 + 64)
            b_one = b_ref[rows, thin]
            c_one = c_ref[rows, thin]
            dxi = None
            if c < chunks - 1:
                hi, lo = split(grad[g])
                dxi = dot(
                    jnp.concatenate([b_one, b_one], axis=1),
                    jnp.concatenate([hi, lo], axis=0),
                    1,
                    0,
                )
                dxi = dxi * weight[c, :, wide]
                dbi = cross(xh[c, :, wide], xl[c, :, wide], grad[g])
            scores = dot(b_one, c_one, 1, 1)
            total = jnp.zeros((CH, CH), F32)
            for k in range(4):
                lanes = slice(g * 512 + k * 128, g * 512 + k * 128 + 128)
                dy = dy_c[:, lanes]
                zero = jnp.zeros_like(dy)
                stacked = jnp.concatenate(
                    [jnp.where(first, dy, zero), jnp.where(first, zero, dy)], axis=0
                )
                pairs = dot(x_ref[rows, lanes], stacked, 1, 1)
                his, los = [], []
                for e in range(2):
                    h = g * 8 + 2 * k + e
                    gap = cum_t[h : h + 1, :] - jnp.broadcast_to(cum_s[:, h : h + 1], (CH, CH))
                    decay = jnp.exp2(jnp.where(causal, gap, -jnp.inf))
                    decay = decay * jnp.broadcast_to(rate_s[:, h : h + 1], (CH, CH))
                    total = total + decay * pairs[:, e * CH : (e + 1) * CH]
                    hi, lo = split(decay * scores)
                    his.append(hi)
                    los.append(lo)
                lhs = jnp.concatenate(
                    [jnp.concatenate(his, axis=1), jnp.concatenate(los, axis=1)], axis=0
                )
                res = dot(lhs, stacked, 1, 0)
                dx = res[0:CH] + res[CH : 2 * CH]
                if dxi is not None:
                    dx = dx + dxi[:, k * 128 : k * 128 + 128]
                dx_ref[rows, lanes] = dx.astype(dx_ref.dtype)
            hi, lo = split(total)
            db = dot(hi, c_one, 1, 0) + dot(lo, c_one, 1, 0)
            dc = dot(hi, b_one, 0, 0) + dot(lo, b_one, 0, 0)
            if c < chunks - 1:
                db = db + dbi
            if c > 0:
                dc = dc + dci[c, g]
            if c == chunks - 1:
                grad[g] = carry[c, g]
            elif c > 0 or carry_ref is not None:
                grad[g] = ends[c][:, wide] * grad[g] + carry[c, g]
            db_ref[rows, thin] = db.astype(db_ref.dtype)
            dc_ref[rows, thin] = dc
    if carry_ref is not None:
        for g in range(2):
            for q in range(2):
                carry_ref[2 * g + q] = grad[g][:, q * 256 : q * 256 + 256]


def inside(length, x, dy, b, c, dt, upto, rest, kind, after, micros, name):
    n = x.shape[0]
    chunks = n // CH

    def scratch(dtype):
        return pltpu.VMEM((chunks, CH, 1024), dtype)

    has_length = length is not None
    return call(
        functools.partial(inside_kernel, chunks, has_length),
        [SMEM] * has_length + [cols(n, 1024)] * 2 + [cols(n, 128)] * 2 + [heads(n)] * 3,
        (cols(n, 1024), cols(n, 128), cols(n, 128))
        + (() if has_length else (pl.BlockSpec((4, 64, 256), lambda i: (i, 0, 0)),)),
        (
            jax.ShapeDtypeStruct(x.shape, kind),
            jax.ShapeDtypeStruct(b.shape, kind),
            jax.ShapeDtypeStruct(c.shape, F32),
        )
        + (() if has_length else (jax.ShapeDtypeStruct((16, 64, 256), F32),)),
        (*([length] if has_length else []), x, dy, b, c, dt, upto, rest),
        after,
        grid=(4,),
        scratch_shapes=[scratch(BF16)] * 4 + [scratch(F32)],
        compiler_params=limits(MOST if has_length else BIG),
        cost_estimate=cost(micros),
        name=name,
    )


def diagonal(ref, q, j):
    pair = ref[q, :, j * 128 : j * 128 + 128]
    first = halves(64)
    hi, lo = split(pair)
    zero = jnp.zeros_like(hi)
    rows = [jnp.where(first, v, zero) if h == 0 else jnp.where(first, zero, v) for v in (hi, lo) for h in (0, 1)]
    return jnp.concatenate(rows, axis=0)


def product(value, state, weight):
    res = dot(value, state, 1, 1)
    return (res[:, 0:128] + res[:, 128:256]) * weight


def start_kernel(base, dy_ref, e_ref, state_ref, part_ref, dc_ref):
    state_ref = state_ref.at[:, base : base + 64, :]
    e_turned = e_ref[0]
    pick = picker()
    out = []
    for g in range(2):
        total = None
        for q in (2 * g, 2 * g + 1):
            e = dot(e_turned, pick[:, q * 256 : q * 256 + 256], 1, 0)
            for j in range(2):
                lanes = slice(q * 256 + j * 128, q * 256 + j * 128 + 128)
                term = product(dy_ref[:, lanes], diagonal(state_ref, q, j), e[:, j * 128 : j * 128 + 128])
                total = term if total is None else total + term
        out.append(total[:, 0:64] + total[:, 64:128])
    dc_ref[...] = (part_ref[...] + jnp.concatenate(out, axis=1)).astype(BF16)


def from_start(dy, e, states, base, part, after, name):
    n = dy.shape[0]
    return call(
        functools.partial(start_kernel, base),
        [cols(n, 1024), turns(n)]
        + [pl.BlockSpec((4,) + states.shape[1:], lambda i: (i, 0, 0)), cols(n, 128)],
        (cols(n, 128),),
        (jax.ShapeDtypeStruct((n, 512), BF16),),
        (dy, e, states, part),
        after,
        grid=(4,),
        compiler_params=limits(MOST),
        cost_estimate=cost(n / 64),
        name=name,
    )


def end_kernel(base, x_ref, b_ref, w_ref, state_ref, dxp_ref, dbp_ref, dx_ref, db_ref):
    state_ref = state_ref.at[:, base : base + 64, :]
    w_turned = w_ref[0]
    pick = picker()
    out = []
    for g in range(2):
        total = None
        b_one = b_ref[:, g * 64 : g * 64 + 64]
        b_two = jnp.concatenate([b_one, b_one], axis=1)
        for q in (2 * g, 2 * g + 1):
            wide = slice(q * 256, q * 256 + 256)
            w = dot(w_turned, pick[:, wide], 1, 0)
            hi, lo = split(state_ref[q])
            dx = dot(b_two, jnp.concatenate([hi, lo], axis=0), 1, 0) * w
            dx_ref[:, wide] = (dxp_ref[:, wide] + dx).astype(BF16)
            for j in range(2):
                lanes = slice(q * 256 + j * 128, q * 256 + j * 128 + 128)
                term = product(x_ref[:, lanes], diagonal(state_ref, q, j), w[:, j * 128 : j * 128 + 128])
                total = term if total is None else total + term
        out.append(total[:, 0:64] + total[:, 64:128])
    db_ref[...] = (dbp_ref[...] + jnp.concatenate(out, axis=1)).astype(BF16)


def tail_kernel(
    x_ref, b_ref, w_ref, state_ref, dxp_ref, dbp_ref, ydy_ref, ye_ref, ydcp_ref, dx_ref, db_ref, ydc_ref
):
    end_kernel(0, x_ref, b_ref, w_ref, state_ref, dxp_ref, dbp_ref, dx_ref, db_ref)
    start_kernel(64, ydy_ref, ye_ref, state_ref, ydcp_ref, ydc_ref)


def from_states(x, b, w, states, dx_part, db_part, ydy, ye, ydc_part):
    n, m = x.shape[0], ydy.shape[0]
    wide = lambda k: pl.BlockSpec((k // 2, 1024), lambda i, j: (j, i))
    thin = lambda k: pl.BlockSpec((k // 2, 128), lambda i, j: (j, i))
    turned_half = lambda k: pl.BlockSpec((1, k // 2, 32), lambda i, j: (i, j, 0))
    return call(
        tail_kernel,
        [wide(n), thin(n), turned_half(n)]
        + [pl.BlockSpec((4, 128, 256), lambda i, j: (i, 0, 0)), wide(n), thin(n)]
        + [wide(m), turned_half(m), thin(m)],
        (wide(n), thin(n), thin(m)),
        (
            jax.ShapeDtypeStruct(x.shape, BF16),
            jax.ShapeDtypeStruct(b.shape, BF16),
            jax.ShapeDtypeStruct((m, 512), BF16),
        ),
        (x, b, w, states, dx_part, db_part, ydy, ye, ydc_part),
        grid=(4, 2),
        compiler_params=limits(MOST),
        cost_estimate=cost(12),
        name="from_states",
    )


def local(
    prompt_x,
    prompt_dt,
    head_rate,
    prompt_b,
    prompt_c,
    prompt_dy,
    branch_x,
    branch_dt,
    branch_b,
    branch_c,
    branch_dy,
    parent,
    lengths,
):
    x, dy, b, c = prompt_x[0], prompt_dy[0], prompt_b[0], prompt_c[0]
    yx, ydy, yb, yc = branch_x[0], branch_dy[0], branch_b[0], branch_c[0]
    dt, ydt = prompt_dt[0].T, branch_dt[0].T
    rate = head_rate[None, :]
    leaf = lax.axis_index("leaf")
    place = jnp.stack([leaf // 2, leaf % 2]).astype(jnp.int32)
    swap = [(s, s ^ 1) for s in range(8)]

    def turn(value):
        return lax.all_to_all(value, "seq", 0, 0, tiled=True)

    sent, upto, rest, yupto, yrest, e, w, ye = first_message(lengths, parent, rate, x, b, dt, ydy, yc, ydt)
    got = turn(sent)
    dx_part, db_part, dc_part, csent = inside(
        None, x, dy, b, c, dt, upto, rest, F32, (sent,), 28, "prompt_inside"
    )
    second, end = forward(got, csent, ())
    back = turn(second)
    keep, send = buckets(place, got, end)
    recv = lax.ppermute(send, "leaf", swap)
    m1, m2, m3, own = pack(place, end, keep, recv)
    received = [
        lax.ppermute(m, "leaf", [(s, (s + 2 * d) % 8) for s in range(8)])
        for d, m in ((1, m1), (2, m2), (3, m3))
    ]
    (third,) = backward(place, got, back, end, recv, own, received)
    states = turn(third)
    (dc,) = from_start(dy, e, back, 64, dc_part, (third,), "prompt_from_start")
    ydx, ydb, ydc_part = inside(
        lengths, yx, ydy, yb, yc, ydt, yupto, yrest, BF16, (dc,), 14, "branch_inside"
    )
    dx, db, ydc = from_states(x, b, w, states, dx_part, db_part, ydy, ye, ydc_part)
    return tuple(a[None] for a in (dx, db, dc, ydx, ydb, ydc))


def solution(mesh):
    seq = P("leaf", "seq", None)
    own = P(("seq", "leaf"), None, None)
    ids = P(("seq", "leaf"))
    in_specs = (seq, seq, P(), seq, seq, seq, own, own, own, own, own, ids, ids)
    out_specs = (seq, seq, seq, own, own, own)
    return jax.shard_map(local, mesh=mesh, in_specs=in_specs, out_specs=out_specs, check_vma=False)
```
